512 devices in a mesh: tile: 8 (over y, core), depth: 64 (over x, z).
Axes of the slice: x: 4, y: 4, z: 16, core: 2. Of those that a mesh axis runs over, the one named last changes fastest.
Arguments:
- density: float32 [128, 2048, 2048], P('tile', 'depth'), may hold values from 0.2 to 3
- slab_start: int32 [16, 64, 16], P('tile', 'depth'), may hold values from 0 to 31, as said below
- slab_count: int32 [16, 64, 16], P('tile', 'depth'), may hold values from 1 to 32
- emission: float32 [3], replicated, may hold values from 0.5 to 2
- extinction: float32 [1], replicated, may hold values from 1 to 4
- edge_gain: float32 [1], replicated, may hold values from 0.25 to 1
Outputs:
- image: float32 [4, 128, 2048], P(None, 'tile')
The draws below stay inside these ranges and needn't reach their ends.
Inputs may be any that keep to these rules, and one draw needn't show every extreme that they name: `slab_start`: start + count of each brick is at most 32.
All inputs are finite; a program needn't handle non-finite values.
Results may differ from the reference program's by a relative error of at most 0.0003.
Values sent between devices are 32-bit elements; how exact they have to be, the bound alone decides.
A program may use at most 128 MiB of HBM per device.

```python
import math
import jax
import jax.numpy as jnp
from jax import lax

W = 2048
SLICES = 32
BR = 8
BW = 128
H = 128
NZ = 2048
N_DEPTH = 64


def brick_ranges(key):
    shape = (H // BR, N_DEPTH, W // BW)
    key_coin, key_dense, key_sparse, key_start = jax.random.split(key, 4)
    coin = jax.random.randint(key_coin, (H // BR, N_DEPTH, 1), 0, 3)
    dense = jnp.minimum(jax.random.randint(key_dense, shape, 1, 2 * SLICES + 1), SLICES)
    sparse = jax.random.randint(key_sparse, shape, 1, SLICES // 4 + 2)
    count = jnp.where(coin > 0, dense, sparse).astype(jnp.int32)
    start = jax.random.randint(key_start, shape, 0, SLICES - count + 1).astype(jnp.int32)
    return (start, count)


def draw_slab_start(key, part):
    return brick_ranges(key)[0]


def draw_slab_count(key, part):
    return brick_ranges(key)[1]


def block_scale(stream_key, extent, cuts, smallest, top_value):
    factor_of, own = 1.0, jax.random.fold_in(stream_key, 6)
    for dim, parts in cuts:
        heights = jnp.exp(jax.random.uniform(jax.random.fold_in(own, dim), (parts,), jnp.float32, smallest / len(cuts), top_value / len(cuts)))
        factor_of = factor_of * jnp.repeat(heights, extent[dim] // parts).reshape([-1 if axis == dim else 1 for axis in range(len(extent))])
    return factor_of


def setup_inputs(seed: int = 0) -> dict:
    streams_of = jax.random.split(jax.random.key(seed), 7)
    density = jnp.clip(jnp.exp(math.log(3.0) - 2.7080502 * jax.random.uniform(streams_of[0], (H, NZ, W), jnp.float32) ** block_scale(streams_of[0], (H, NZ, W), ((0, 8), (1, 64)), -0.2, 0.2)), 0.2, 3.0)
    slab_start = draw_slab_start(jax.random.fold_in(streams_of[6], 71), 0)
    slab_count = draw_slab_count(jax.random.fold_in(streams_of[6], 71), 0)
    emission = jnp.clip(jnp.exp(jax.random.uniform(streams_of[3], (3,), jnp.float32, math.log(0.5), math.log(2.0))), 0.5, 2.0)
    extinction = jnp.clip(jnp.exp(jax.random.uniform(streams_of[4], (1,), jnp.float32, math.log(1.0), math.log(4.0))), 1.0, 4.0)
    edge_gain = jnp.clip(jnp.exp(jax.random.uniform(streams_of[5], (1,), jnp.float32, math.log(0.25), math.log(1.0))), 0.25, 1.0)
    return {"density": density, "slab_start": slab_start, "slab_count": slab_count, "emission": emission, "extinction": extinction, "edge_gain": edge_gain}


def expand_table(table):
    return jnp.repeat(jnp.repeat(table, BR, axis=0), BW, axis=1)


def reference(density, slab_start, slab_count, emission, extinction, edge_gain):
    slab_end = slab_start + slab_count

    def march(carry, k):
        color, trans = carry
        slab = k // SLICES
        local = k % SLICES
        low = expand_table(lax.dynamic_index_in_dim(slab_start, slab, 1, keepdims=False))
        high = expand_table(lax.dynamic_index_in_dim(slab_end, slab, 1, keepdims=False))
        live = ((low <= local) & (local < high)).astype(jnp.float32)
        dens = lax.dynamic_index_in_dim(density, k, 1, keepdims=False)
        padded = jnp.pad(dens, 1)
        grad_y = (padded[2:, 1:-1] - padded[:-2, 1:-1]) * 0.5
        grad_x = (padded[1:-1, 2:] - padded[1:-1, :-2]) * 0.5
        source = dens + edge_gain[0] * (grad_y * grad_y + grad_x * grad_x)
        tau = extinction[0] * dens * live / NZ
        keep = jnp.exp(-tau)
        weight = trans * (1.0 - keep) * source
        color = color + weight[None] * emission[:, None, None]
        trans = trans * keep
        return (color, trans), None

    init = (jnp.zeros((3, H, W), jnp.float32), jnp.ones((H, W), jnp.float32))
    (color, trans), _ = lax.scan(march, init, jnp.arange(NZ, dtype=jnp.int32))
    return jnp.concatenate([color, (1.0 - trans)[None]], axis=0)
```

```python
import functools
import math

import jax
import jax.numpy as jnp
from jax import lax
from jax.experimental import pallas as pl
from jax.experimental.pallas import tpu as pltpu
from jax.sharding import PartitionSpec as P

MESH = pl.DeviceIdType.MESH
BR, BW = 8, 128


def render(
    nt, nx, nz, density, start, count, emission, extinction, edge_gain, image,
    field, states, parts, mixed, crossed, pieces,
    load_sem, halo_send, halo_recv, z_send, z_recv, x_send, x_recv, g_send, g_recv, f_send, f_recv,
):
    rows, slices, width = density.shape
    blocks = width // BW
    bricks = rows // BR
    tile = lax.axis_index("tile")
    place = lax.axis_index("depth")
    x, z = place // nz, lax.rem(place, nz)

    def at(px, pz):
        return (tile, px * nz + pz)

    barrier = pltpu.get_barrier_semaphore()

    def greet_z(j, _):
        pl.semaphore_signal(barrier, inc=1, device_id=at(x, lax.rem(z + j, nz)), device_id_type=MESH)
        return 0

    def greet_x(j, _):
        pl.semaphore_signal(barrier, inc=1, device_id=at(lax.rem(x + j, nx), z), device_id_type=MESH)
        return 0

    above = lax.rem(tile + nt - 1, nt)
    below = lax.rem(tile + 1, nt)
    pl.semaphore_signal(barrier, inc=1, device_id=(above, place), device_id_type=MESH)
    pl.semaphore_signal(barrier, inc=1, device_id=(below, place), device_id_type=MESH)
    lax.fori_loop(1, nz, greet_z, 0)
    lax.fori_loop(1, nx, greet_x, 0)

    def load(b):
        return pltpu.make_async_copy(
            density.at[:, :, pl.ds(pl.multiple_of(b * BW, BW), BW)],
            field.at[b + 1, pl.ds(1, rows)],
            load_sem.at[b],
        )

    def start_load(b, _):
        load(b).start()
        return 0

    lax.fori_loop(0, blocks, start_load, 0)
    zeros = jnp.zeros((rows + 2, slices, BW), jnp.float32)
    field[0] = zeros
    field[blocks + 1] = zeros

    def turn(i):
        gap = (blocks // 2) - (i + 1) // 2
        side = jnp.where(lax.rem(i, 2) == 1, blocks - gap, gap)
        return lax.rem(z + side, blocks)

    pl.semaphore_wait(barrier, nz - 1 + nx - 1 + 2)

    def halo_up(b):
        return pltpu.make_async_remote_copy(
            density.at[0, :, pl.ds(pl.multiple_of(b * BW, BW), BW)],
            field.at[b + 1, rows + 1],
            halo_send.at[0, b],
            halo_recv.at[0, b],
            device_id=(above, place),
            device_id_type=MESH,
        )

    def halo_down(b):
        return pltpu.make_async_remote_copy(
            density.at[rows - 1, :, pl.ds(pl.multiple_of(b * BW, BW), BW)],
            field.at[b + 1, 0],
            halo_send.at[1, b],
            halo_recv.at[1, b],
            device_id=(below, place),
            device_id_type=MESH,
        )

    def start_halo(i, _):
        b = turn(i)
        halo_up(b).start()
        halo_down(b).start()
        return 0

    lax.fori_loop(0, blocks, start_halo, 0)

    def end_load(b, _):
        load(b).wait()
        return 0

    lax.fori_loop(0, blocks, end_load, 0)

    lane = lax.broadcasted_iota(jnp.int32, (BR, BW), 1)
    first_lane, last_lane = lane == 0, lane == BW - 1
    sub = lax.broadcasted_iota(jnp.int32, (BR, BW), 0)
    rate = extinction[0] * (-math.log2(math.e) / (slices * nx * nz))
    gain = edge_gain[0] * 0.25
    top = jnp.where(tile == 0, 0.0, 1.0)
    bottom = jnp.where(tile == nt - 1, 0.0, 1.0)
    weight_up = jnp.where(sub == 0, top, 1.0)
    weight_down = jnp.where(sub == BR - 1, bottom, 1.0)

    def march(b):
        flat = [field.at[b + j].reshape((rows + 2) * slices, BW) for j in range(3)]

        def step(k, carry):
            out = []
            for h in range(bricks):
                total, trans, color = carry[h]
                base = (BR * h + 1) * slices + k
                left, mid, right = (f[pl.ds(base, BR, stride=slices)] for f in flat)
                up = flat[1][pl.ds(base - slices, BR, stride=slices)]
                down = flat[1][pl.ds(base + slices, BR, stride=slices)]
                if h == 0:
                    up = up * weight_up
                if h == bricks - 1:
                    down = down * weight_down
                before = pltpu.roll(jnp.where(last_lane, left, mid), 1, 1)
                after = pltpu.roll(jnp.where(first_lane, right, mid), BW - 1, 1)
                grad_y, grad_x = down - up, after - before
                source = mid + gain * (grad_y * grad_y + grad_x * grad_x)
                low = start[h, 0, b]
                live = jnp.logical_and(low <= k, k < low + count[h, 0, b])
                total = total + jnp.where(live, rate, 0.0) * mid
                later = jnp.exp2(total)
                out.append((total, later, color + (trans - later) * source))
            return tuple(out)

        zero, one = jnp.zeros((BR, BW), jnp.float32), jnp.ones((BR, BW), jnp.float32)
        done = lax.fori_loop(0, slices, step, ((zero, one, zero),) * bricks, unroll=8)
        return [(color, trans) for _, trans, color in done]

    def z_copy(b):
        return pltpu.make_async_remote_copy(
            states.at[b], parts.at[z], z_send.at[b], z_recv.at[z], device_id=at(x, b), device_id_type=MESH
        )

    def one_block(i, _):
        b = turn(i)
        halo_up(b).wait_recv()
        halo_down(b).wait_recv()
        for h, (color, trans) in enumerate(march(b)):
            states[b, 2 * h] = color
            states[b, 2 * h + 1] = trans

        @pl.when(i < blocks - 1)
        def _():
            z_copy(b).start()

        return 0

    lax.fori_loop(0, blocks, one_block, 0)
    parts[z] = states[z]

    def arrived(j, _):
        @pl.when(j != z)
        def _():
            pltpu.make_async_remote_copy(
                states.at[j], parts.at[j], z_send.at[j], z_recv.at[j], device_id=at(x, j), device_id_type=MESH
            ).wait_recv()

        return 0

    lax.fori_loop(0, nz, arrived, 0)

    def over(j, carry):
        out = []
        for h in range(bricks):
            color, trans = carry[h]
            out.append((color + trans * parts[j, 2 * h], trans * parts[j, 2 * h + 1]))
        return tuple(out)

    zero, one = jnp.zeros((BR, BW), jnp.float32), jnp.ones((BR, BW), jnp.float32)
    merged = lax.fori_loop(0, nz, over, ((zero, one),) * bricks)

    half = BR // 2
    upper = sub < half
    for h, (color, trans) in enumerate(merged):
        mixed[2 * h] = jnp.where(upper, color, pltpu.roll(trans, half, 0))
        mixed[2 * h + 1] = jnp.where(upper, pltpu.roll(color, half, 0), trans)

    def x_copy(j):
        other = lax.rem(x + j, nx)
        return pltpu.make_async_remote_copy(
            mixed.at[other], crossed.at[x], x_send.at[j], x_recv.at[x], device_id=at(other, z), device_id_type=MESH
        )

    for j in range(1, nx):
        x_copy(j).start()
    crossed[x] = mixed[x]
    for j in range(1, nx):
        other = lax.rem(x + j, nx)
        pltpu.make_async_remote_copy(
            mixed.at[x], crossed.at[other], x_send.at[j], x_recv.at[other], device_id=at(other, z), device_id_type=MESH
        ).wait_recv()
    final = crossed[0]
    for j in range(1, nx):
        nearer = jnp.where(upper, pltpu.roll(final, half, 0), final)
        final = jnp.where(upper, final, 0.0) + nearer * crossed[j]
    pieces[x, z] = final

    def g_copy(j):
        return pltpu.make_async_remote_copy(
            pieces.at[x, z], pieces.at[x, z], g_send.at[j], g_recv.at[z],
            device_id=at(x, lax.rem(z + j, nz)), device_id_type=MESH,
        )

    def start_g(j, _):
        g_copy(j).start()
        return 0

    lax.fori_loop(1, nz, start_g, 0)

    def wait_g(j, _):
        other = lax.rem(z + j, nz)
        pltpu.make_async_remote_copy(
            pieces.at[x, other], pieces.at[x, other], g_send.at[j], g_recv.at[other],
            device_id=at(x, other), device_id_type=MESH,
        ).wait_recv()
        return 0

    lax.fori_loop(1, nz, wait_g, 0)

    def f_copy(j):
        return pltpu.make_async_remote_copy(
            pieces.at[x], pieces.at[x], f_send.at[j], f_recv.at[x],
            device_id=at(lax.rem(x + j, nx), z), device_id_type=MESH,
        )

    for j in range(1, nx):
        f_copy(j).start()
    for j in range(1, nx):
        other = lax.rem(x + j, nx)
        pltpu.make_async_remote_copy(
            pieces.at[other], pieces.at[other], f_send.at[j], f_recv.at[other],
            device_id=at(other, z), device_id_type=MESH,
        ).wait_recv()

    for b in range(blocks):
        for h in range(bricks):
            first, second = pieces[2 * h, b], pieces[2 * h + 1, b]
            color = jnp.where(upper, first, pltpu.roll(second, half, 0))
            trans = jnp.where(upper, pltpu.roll(first, half, 0), second)
            spot = (pl.ds(BR * h, BR), pl.ds(BW * b, BW))
            for c in range(3):
                image[(c,) + spot] = emission[c] * color
            image[(3,) + spot] = 1.0 - trans

    def end_halo(b, _):
        halo_up(b).wait_send()
        halo_down(b).wait_send()
        return 0

    def end_z(j, _):
        z_copy(lax.rem(z + j, nz)).wait_send()
        g_copy(j).wait_send()
        return 0

    lax.fori_loop(0, blocks, end_halo, 0)
    lax.fori_loop(1, nz, end_z, 0)
    for j in range(1, nx):
        x_copy(j).wait_send()
        f_copy(j).wait_send()


def shards(nt, nx, nz, density, slab_start, slab_count, emission, extinction, edge_gain):
    rows, slices, width = density.shape
    blocks, bricks = width // BW, rows // BR
    vmem, smem, anywhere = (pl.BlockSpec(memory_space=m) for m in (pltpu.VMEM, pltpu.SMEM, pl.ANY))
    dma = pltpu.SemaphoreType.DMA
    return pl.pallas_call(
        functools.partial(render, nt, nx, nz),
        out_shape=jax.ShapeDtypeStruct((4, rows, width), jnp.float32),
        in_specs=[anywhere] + [smem] * 5,
        out_specs=vmem,
        scratch_shapes=[
            pltpu.VMEM((blocks + 2, rows + 2, slices, BW), jnp.float32),
            pltpu.VMEM((blocks, 2 * bricks, BR, BW), jnp.float32),
            pltpu.VMEM((nz, 2 * bricks, BR, BW), jnp.float32),
            pltpu.VMEM((nx, BR, BW), jnp.float32),
            pltpu.VMEM((nx, BR, BW), jnp.float32),
            pltpu.VMEM((nx, nz, BR, BW), jnp.float32),
            dma((blocks,)),
            dma((2, blocks)),
            dma((2, blocks)),
            dma((blocks,)),
            dma((nz,)),
            dma((nx,)),
            dma((nx,)),
            dma((nz,)),
            dma((nz,)),
            dma((nx,)),
            dma((nx,)),
        ],
        compiler_params=pltpu.CompilerParams(
            collective_id=0, has_side_effects=True, vmem_limit_bytes=32 * 1024 * 1024
        ),
        name="render",
    )(density, slab_start, slab_count, emission, extinction, edge_gain)


def solution(mesh):
    placed = (
        P("tile", "depth", None),
        P("tile", "depth", None),
        P("tile", "depth", None),
        P(),
        P(),
        P(),
    )
    nt, nd = mesh.shape["tile"], mesh.shape["depth"]
    nz = 16
    return jax.shard_map(
        functools.partial(shards, nt, nd // nz, nz),
        mesh=mesh,
        in_specs=placed,
        out_specs=P(None, "tile", None),
        check_vma=False,
    )
```

```python
import functools
import math

import jax
import jax.numpy as jnp
from jax import lax
from jax.experimental import pallas as pl
from jax.experimental.pallas import tpu as pltpu
from jax.sharding import PartitionSpec as P

MESH = pl.DeviceIdType.MESH
BR, BW = 8, 128
HALF = BR // 2
PAD = 8
NEAR = 4


def render(
    nt, nx, nz, density, start_in, count_in, emission_in, extinction_in, edge_gain_in, image,
    start, count, emission, extinction, edge_gain, field, states, parts, pieces,
    small_sem, load_sem, halo_send, halo_recv, near_sem, far_sem, r_send, r_recv, g_send, g_recv, f_send, f_recv, o_sem,
):
    rows, slices, width = density.shape
    blocks = width // BW
    bricks = rows // BR
    tile = lax.axis_index("tile")
    place = lax.axis_index("depth")
    x, z = place // nz, lax.rem(place, nz)
    has_above, has_below = tile > 0, tile < nt - 1
    above, below = jnp.where(has_above, tile - 1, tile + 1), jnp.where(has_below, tile + 1, tile - 1)

    def at(px, pz):
        return (tile, px * nz + pz)

    def along(dz):
        return lax.rem(z + dz + nz, nz)

    barrier = pltpu.get_barrier_semaphore()
    reach = NEAR // 2

    @pl.when(has_above)
    def _():
        pl.semaphore_signal(barrier, inc=1, device_id=(above, place), device_id_type=MESH)

    @pl.when(has_below)
    def _():
        pl.semaphore_signal(barrier, inc=1, device_id=(below, place), device_id_type=MESH)

    for dz in range(-reach, reach + 1):
        for dx in range(nx):
            if dx or dz:
                pl.semaphore_signal(
                    barrier, inc=1, device_id=at(lax.rem(x + dx, nx), along(dz)), device_id_type=MESH
                )

    small = [
        pltpu.make_async_copy(source, target, small_sem.at[i])
        for i, (source, target) in enumerate((
            (start_in, start), (count_in, count), (emission_in, emission),
            (extinction_in, extinction), (edge_gain_in, edge_gain),
        ))
    ]
    for copy in small:
        copy.start()

    def load(b):
        return pltpu.make_async_copy(
            density.at[:, :, pl.ds(pl.multiple_of(b * BW, BW), BW)],
            field.at[b + 1, pl.ds(1, rows), pl.ds(0, slices)],
            load_sem.at[b],
        )

    def start_load(b, _):
        load(b).start()
        return 0

    lax.fori_loop(0, blocks, start_load, 0)
    zeros = jnp.zeros((rows + 2, slices + PAD, BW), jnp.float32)
    field[0] = zeros
    field[blocks + 1] = zeros
    edge = jnp.zeros((blocks, slices, BW), jnp.float32)

    @pl.when(jnp.logical_not(has_above))
    def _():
        field[pl.ds(1, blocks), 0, pl.ds(0, slices)] = edge

    @pl.when(jnp.logical_not(has_below))
    def _():
        field[pl.ds(1, blocks), rows + 1, pl.ds(0, slices)] = edge


    def turn(i):
        gap = jnp.where(i < 2 * NEAR, NEAR - i // 2, 2 * NEAR - (i - 2 * NEAR + 1) // 2)
        gap = jnp.where(i == blocks - 1, 0, gap)
        return lax.rem(z + jnp.where(lax.rem(i, 2) == 1, nz - gap, gap), nz)

    def halo_up(b):
        return pltpu.make_async_remote_copy(
            density.at[0, :, pl.ds(pl.multiple_of(b * BW, BW), BW)],
            field.at[b + 1, rows + 1, pl.ds(0, slices)],
            halo_send.at[0, b],
            halo_recv.at[0, b],
            device_id=(above, place),
            device_id_type=MESH,
        )

    def halo_down(b):
        return pltpu.make_async_remote_copy(
            density.at[rows - 1, :, pl.ds(pl.multiple_of(b * BW, BW), BW)],
            field.at[b + 1, 0, pl.ds(0, slices)],
            halo_send.at[1, b],
            halo_recv.at[1, b],
            device_id=(below, place),
            device_id_type=MESH,
        )

    def start_halo(i, _):
        b = turn(i)

        @pl.when(has_above)
        def _():
            halo_up(b).start()

        @pl.when(has_below)
        def _():
            halo_down(b).start()

        return 0

    pl.semaphore_wait(barrier, nx * (2 * reach + 1) + jnp.where(jnp.logical_and(has_above, has_below), 1, 0))
    for dz in (-reach, reach):
        pl.semaphore_signal(near_sem, inc=1, device_id=at(x, along(dz)), device_id_type=MESH)
    lax.fori_loop(0, blocks, start_halo, 0)
    pl.semaphore_wait(near_sem, 2)
    for dz in (-NEAR, NEAR):
        pl.semaphore_signal(far_sem, inc=1, device_id=at(x, along(dz)), device_id_type=MESH)

    def end_load(b, _):
        load(b).wait()
        return 0

    lax.fori_loop(0, blocks, end_load, 0)
    for copy in small:
        copy.wait()

    lane = lax.broadcasted_iota(jnp.int32, (BR, BW), 1)
    first_lane, last_lane = lane == 0, lane == BW - 1
    sub = lax.broadcasted_iota(jnp.int32, (BR, BW), 0)
    upper = sub < HALF
    rate = extinction[0] * (-math.log2(math.e) / (slices * nx * nz))
    gain = edge_gain[0] * 0.25
    zero, one = jnp.zeros((BR, BW), jnp.float32), jnp.ones((BR, BW), jnp.float32)

    def march(b):
        stride = slices + PAD
        flat = [field.at[b + j].reshape((rows + 2) * stride, BW) for j in range(3)]
        ranges = [(start[h, 0, b], start[h, 0, b] + count[h, 0, b]) for h in range(bricks)]

        def step(k, carry):
            result = []
            for h in range(bricks):
                total, trans, color = carry[h]
                base = (BR * h + 1) * stride + k
                left, mid, right = (f[pl.ds(base, BR, stride=stride)] for f in flat)
                up = flat[1][pl.ds(base - stride, BR, stride=stride)]
                down = flat[1][pl.ds(base + stride, BR, stride=stride)]
                before = pltpu.roll(jnp.where(last_lane, left, mid), 1, 1)
                after = pltpu.roll(jnp.where(first_lane, right, mid), BW - 1, 1)
                grad_y, grad_x = down - up, after - before
                source = mid + gain * (grad_y * grad_y + grad_x * grad_x)
                low, high = ranges[h]
                live = jnp.logical_and(low <= k, k < high)
                total = total + jnp.where(live, rate, 0.0) * mid
                later = jnp.exp2(total)
                result.append((total, later, color + (trans - later) * source))
            return tuple(result)

        done = lax.fori_loop(0, slices, step, ((zero, one, zero),) * bricks, unroll=slices)
        return [(color, trans) for _, trans, color in done]

    def r_copy(q, b):
        return pltpu.make_async_remote_copy(
            states.at[b, q], parts.at[place], r_send.at[b, q], r_recv, device_id=at(q, b), device_id_type=MESH
        )

    def one_block(i, _):
        b = turn(i)

        @pl.when(has_below)
        def _():
            halo_up(b).wait_recv()

        @pl.when(has_above)
        def _():
            halo_down(b).wait_recv()

        for h, (color, trans) in enumerate(march(b)):
            states[b, 2 * h] = jnp.where(upper, color, pltpu.roll(trans, HALF, 0))
            states[b, 2 * h + 1] = jnp.where(upper, pltpu.roll(color, HALF, 0), trans)
        return b

    def sent_block(i, _):
        b = one_block(i, 0)
        for q in range(nx):
            r_copy(q, b).start()
        return 0

    lax.fori_loop(0, 2 * NEAR, sent_block, 0)
    pl.semaphore_wait(far_sem, 2)
    lax.fori_loop(2 * NEAR, blocks - 1, sent_block, 0)
    one_block(blocks - 1, 0)
    for j in range(1, nx):
        r_copy(lax.rem(x + j, nx), z).start()
    parts[place] = states[z, x]

    others = pl.ds(0, nx * nz - 1)
    pltpu.make_async_remote_copy(
        parts.at[others], parts.at[others], o_sem, r_recv, device_id=at(lax.rem(x + 1, nx), z), device_id_type=MESH
    ).wait_recv()

    def over(j, carry):
        color, trans = carry
        part = parts[j]
        both = jnp.where(upper, pltpu.roll(part, HALF, 0), part)
        return color + trans * part, trans * both

    color, trans = lax.fori_loop(0, nx * nz, over, (zero, one), unroll=nz)
    pieces[x, z] = jnp.where(upper, color, trans)

    def g_copy(j):
        return pltpu.make_async_remote_copy(
            pieces.at[x, z], pieces.at[x, z], g_send.at[j], g_recv.at[z], device_id=at(x, lax.rem(z + j, nz)), device_id_type=MESH
        )

    def f_copy(j, other):
        return pltpu.make_async_remote_copy(
            pieces.at[x, other], pieces.at[x, other], f_send.at[j], f_recv.at[x],
            device_id=at(lax.rem(x + j, nx), z), device_id_type=MESH,
        )

    def arrive(i):
        gap = i // 2 + 1
        return jnp.where(lax.rem(i, 2) == 1, nz - gap, gap)

    def start_g(i, _):
        g_copy(arrive(nz - 2 - i)).start()
        return 0

    lax.fori_loop(0, nz - 1, start_g, 0)
    for j in range(1, nx):
        f_copy(j, z).start()

    def pass_on(i, _):
        other = lax.rem(z + arrive(i), nz)
        pltpu.make_async_remote_copy(
            pieces.at[x, other], pieces.at[x, other], g_send.at[other], g_recv.at[other],
            device_id=at(x, other), device_id_type=MESH,
        ).wait_recv()
        for j in range(1, nx):
            f_copy(j, other).start()
        return 0

    lax.fori_loop(0, nz - 1, pass_on, 0)

    def whole(j):
        other = lax.rem(x + j, nx)
        return pltpu.make_async_remote_copy(
            pieces.at[other], pieces.at[other], f_send.at[j], f_recv.at[other],
            device_id=at(other, z), device_id_type=MESH,
        )

    for j in range(1, nx):
        whole(j).wait_recv()

    for b in range(blocks):
        for h in range(bricks):
            first, second = pieces[2 * h, b], pieces[2 * h + 1, b]
            color = jnp.where(upper, first, pltpu.roll(second, HALF, 0))
            trans = jnp.where(upper, pltpu.roll(first, HALF, 0), second)
            spot = (pl.ds(BR * h, BR), pl.ds(BW * b, BW))
            for c in range(3):
                image[(c,) + spot] = emission[c] * color
            image[(3,) + spot] = 1.0 - trans

    def end_halo(b, _):
        @pl.when(has_above)
        def _():
            halo_up(b).wait_send()

        @pl.when(has_below)
        def _():
            halo_down(b).wait_send()

        for q in range(nx):
            @pl.when(jnp.logical_or(q != x, b != z))
            def _():
                r_copy(q, b).wait_send()
        return 0

    def end_g(j, _):
        g_copy(j).wait_send()
        return 0

    lax.fori_loop(0, blocks, end_halo, 0)
    lax.fori_loop(1, nz, end_g, 0)
    for j in range(1, nx):
        whole(j).wait_send()


def shards(nt, nx, nz, density, slab_start, slab_count, emission, extinction, edge_gain):
    rows, slices, width = density.shape
    blocks = width // BW
    hbm = pl.BlockSpec(memory_space=pltpu.HBM)
    dma, plain = pltpu.SemaphoreType.DMA, pltpu.SemaphoreType.REGULAR
    return pl.pallas_call(
        functools.partial(render, nt, nx, nz),
        out_shape=pltpu.VMEM((4, rows, width), jnp.float32),
        in_specs=[hbm] * 6,
        out_specs=pl.BlockSpec(memory_space=pltpu.VMEM),
        scratch_shapes=[
            pltpu.SMEM(slab_start.shape, jnp.int32),
            pltpu.SMEM(slab_count.shape, jnp.int32),
            pltpu.SMEM(emission.shape, jnp.float32),
            pltpu.SMEM(extinction.shape, jnp.float32),
            pltpu.SMEM(edge_gain.shape, jnp.float32),
            pltpu.VMEM((blocks + 2, rows + 2, slices + PAD, BW), jnp.float32),
            pltpu.VMEM((blocks, nx, BR, BW), jnp.float32),
            pltpu.VMEM((nx * nz, BR, BW), jnp.float32),
            pltpu.VMEM((nx, nz, BR, BW), jnp.float32),
            dma((5,)),
            dma((blocks,)),
            dma((2, blocks)),
            dma((2, blocks)),
            plain,
            plain,
            dma((blocks, nx)),
            dma,
            dma((nz,)),
            dma((nz,)),
            dma((nx,)),
            dma((nx,)),
            dma,
        ],
        compiler_params=pltpu.CompilerParams(
            collective_id=0, has_side_effects=True, vmem_limit_bytes=56 * 1024 * 1024
        ),
        name="render",
    )(density, slab_start, slab_count, emission, extinction, edge_gain)


def solution(mesh):
    placed = (
        P("tile", "depth", None),
        P("tile", "depth", None),
        P("tile", "depth", None),
        P(),
        P(),
        P(),
    )
    nt, nd = mesh.shape["tile"], mesh.shape["depth"]
    nz = 16
    return jax.shard_map(
        functools.partial(shards, nt, nd // nz, nz),
        mesh=mesh,
        in_specs=placed,
        out_specs=P(None, "tile", None),
        check_vma=False,
    )
```

```python
import functools
import math

import jax
import jax.numpy as jnp
from jax import lax
from jax.experimental import pallas as pl
from jax.experimental.pallas import tpu as pltpu
from jax.sharding import PartitionSpec as P

MESH = pl.DeviceIdType.MESH
BR, BW = 8, 128
HALF = BR // 2
PAD = 8
REACH = 2


def render(
    nt, nx, nz, density, start_in, count_in, emission_in, extinction_in, edge_gain_in, image,
    start, count, emission, extinction, edge_gain, field, swap_out, swap_in, states, parts, pieces,
    small_sem, load_sem, halo_send, halo_recv, heard, s_send, s_recv, r_send, r_recv, g_send, g_recv, f_send, f_recv, o_sem,
):
    rows, slices, width = density.shape
    blocks = width // BW
    bricks = rows // BR
    tile = lax.axis_index("tile")
    place = lax.axis_index("depth")
    x, z = place // nz, lax.rem(place, nz)
    groups = nz // 2
    group, member = z // 2, lax.rem(z, 2)
    partner = z + 1 - 2 * member
    has_above, has_below = tile > 0, tile < nt - 1
    above, below = jnp.where(has_above, tile - 1, tile + 1), jnp.where(has_below, tile + 1, tile - 1)

    def at(px, pz):
        return (tile, px * nz + pz)

    def along(dz):
        return lax.rem(z + dz + nz, nz)

    barrier = pltpu.get_barrier_semaphore()

    @pl.when(has_above)
    def _():
        pl.semaphore_signal(barrier, inc=1, device_id=(above, place), device_id_type=MESH)

    @pl.when(has_below)
    def _():
        pl.semaphore_signal(barrier, inc=1, device_id=(below, place), device_id_type=MESH)

    for dz in range(-REACH, REACH + 1):
        for dx in range(nx):
            if dx or dz:
                pl.semaphore_signal(
                    barrier, inc=1, device_id=at(lax.rem(x + dx, nx), along(dz)), device_id_type=MESH
                )

    small = [
        pltpu.make_async_copy(source, target, small_sem.at[i])
        for i, (source, target) in enumerate((
            (start_in, start), (count_in, count), (emission_in, emission),
            (extinction_in, extinction), (edge_gain_in, edge_gain),
        ))
    ]
    for copy in small:
        copy.start()

    def load(b):
        return pltpu.make_async_copy(
            density.at[:, :, pl.ds(pl.multiple_of(b * BW, BW), BW)],
            field.at[b + 1, pl.ds(1, rows), pl.ds(0, slices)],
            load_sem.at[b],
        )

    def start_load(b, _):
        load(b).start()
        return 0

    lax.fori_loop(0, blocks, start_load, 0)
    zeros = jnp.zeros((rows + 2, slices + PAD, BW), jnp.float32)
    field[0] = zeros
    field[blocks + 1] = zeros
    edge = jnp.zeros((blocks, slices, BW), jnp.float32)

    @pl.when(jnp.logical_not(has_above))
    def _():
        field[pl.ds(1, blocks), 0, pl.ds(0, slices)] = edge

    @pl.when(jnp.logical_not(has_below))
    def _():
        field[pl.ds(1, blocks), rows + 1, pl.ds(0, slices)] = edge


    def turn(i):
        gap = groups // 2 - (i + 1) // 2
        return lax.rem(group + jnp.where(lax.rem(i, 2) == 1, gap, groups - gap), groups)

    def block(i):
        return 2 * turn(lax.rem(i, groups)) + jnp.where(i < groups, 1 - member, member)

    def halo_up(b):
        return pltpu.make_async_remote_copy(
            density.at[0, :, pl.ds(pl.multiple_of(b * BW, BW), BW)],
            field.at[b + 1, rows + 1, pl.ds(0, slices)],
            halo_send.at[0],
            halo_recv.at[0, b],
            device_id=(above, place),
            device_id_type=MESH,
        )

    def halo_down(b):
        return pltpu.make_async_remote_copy(
            density.at[rows - 1, :, pl.ds(pl.multiple_of(b * BW, BW), BW)],
            field.at[b + 1, 0, pl.ds(0, slices)],
            halo_send.at[1],
            halo_recv.at[1, b],
            device_id=(below, place),
            device_id_type=MESH,
        )

    def start_halo(i, _):
        b = block(i)

        @pl.when(has_above)
        def _():
            halo_up(b).start()

        @pl.when(has_below)
        def _():
            halo_down(b).start()

        return 0

    pl.semaphore_wait(barrier, nx * (2 * REACH + 1) + jnp.where(jnp.logical_and(has_above, has_below), 1, 0))
    lax.fori_loop(0, blocks, start_halo, 0)
    rounds = [REACH * 2**i for i in range((nz // 2 // REACH).bit_length() - 1)]
    for i, far in enumerate(rounds):
        if i:
            pl.semaphore_wait(heard.at[i - 1], 2)
        for dz in (-far, far):
            pl.semaphore_signal(heard.at[i], inc=1, device_id=at(x, along(dz)), device_id_type=MESH)

    def end_load(b, _):
        load(b).wait()
        return 0

    lax.fori_loop(0, blocks, end_load, 0)
    for copy in small:
        copy.wait()

    lane = lax.broadcasted_iota(jnp.int32, (BR, BW), 1)
    first_lane, last_lane = lane == 0, lane == BW - 1
    sub = lax.broadcasted_iota(jnp.int32, (BR, BW), 0)
    upper = sub < HALF
    rate = extinction[0] * (-math.log2(math.e) / (slices * nx * nz))
    gain = edge_gain[0] * 0.25
    zero, one = jnp.zeros((BR, BW), jnp.float32), jnp.ones((BR, BW), jnp.float32)

    def march(b):
        stride = slices + PAD
        flat = [field.at[b + j].reshape((rows + 2) * stride, BW) for j in range(3)]
        ranges = [(start[h, 0, b], start[h, 0, b] + count[h, 0, b]) for h in range(bricks)]

        def step(k, carry):
            result = []
            for h in range(bricks):
                total, trans, color = carry[h]
                base = (BR * h + 1) * stride + k
                left, mid, right = (f[pl.ds(base, BR, stride=stride)] for f in flat)
                up = flat[1][pl.ds(base - stride, BR, stride=stride)]
                down = flat[1][pl.ds(base + stride, BR, stride=stride)]
                before = pltpu.roll(jnp.where(last_lane, left, mid), 1, 1)
                after = pltpu.roll(jnp.where(first_lane, right, mid), BW - 1, 1)
                grad_y, grad_x = down - up, after - before
                source = mid + gain * (grad_y * grad_y + grad_x * grad_x)
                low, high = ranges[h]
                live = jnp.logical_and(low <= k, k < high)
                total = total + jnp.where(live, rate, 0.0) * mid
                later = jnp.exp2(total)
                result.append((total, later, color + (trans - later) * source))
            return tuple(result)

        done = lax.fori_loop(0, slices, step, ((zero, one, zero),) * bricks, unroll=slices)
        return [(color, trans) for _, trans, color in done]

    def marched(b):
        @pl.when(has_below)
        def _():
            halo_up(b).wait_recv()

        @pl.when(has_above)
        def _():
            halo_down(b).wait_recv()

        return march(b)

    def s_copy(g):
        return pltpu.make_async_remote_copy(
            swap_out.at[g], swap_in.at[g], s_send, s_recv.at[g], device_id=at(x, partner), device_id_type=MESH
        )

    def for_partner(i, _):
        g = turn(i)
        for h, (color, trans) in enumerate(marched(2 * g + 1 - member)):
            swap_out[g, 2 * h] = color
            swap_out[g, 2 * h + 1] = trans
        s_copy(g).start()
        return 0

    def r_copy(q, g):
        return pltpu.make_async_remote_copy(
            states.at[g, q], parts.at[x * groups + group], r_send, r_recv,
            device_id=at(q, 2 * g + member), device_id_type=MESH,
        )

    in_front = member == 0

    def for_owners(i, _):
        g = turn(i)
        mine = marched(2 * g + member)
        s_copy(g).wait_recv()
        for h, (color, trans) in enumerate(mine):
            its_color, its_trans = swap_in[g, 2 * h], swap_in[g, 2 * h + 1]
            color = jnp.where(in_front, color + trans * its_color, its_color + its_trans * color)
            trans = trans * its_trans
            states[g, 2 * h] = jnp.where(upper, color, pltpu.roll(trans, HALF, 0))
            states[g, 2 * h + 1] = jnp.where(upper, pltpu.roll(color, HALF, 0), trans)
        for j in range(1, nx):
            r_copy(lax.rem(x + j, nx), g).start()

        @pl.when(g != group)
        def _():
            r_copy(x, g).start()

        return 0

    lax.fori_loop(0, groups, for_partner, 0)
    pl.semaphore_wait(heard.at[len(rounds) - 1], 2)
    lax.fori_loop(0, groups, for_owners, 0)
    parts[x * groups + group] = states[group, x]

    others = pl.ds(0, nx * groups - 1)
    pltpu.make_async_remote_copy(
        parts.at[others], parts.at[others], o_sem, r_recv, device_id=at(lax.rem(x + 1, nx), z), device_id_type=MESH
    ).wait_recv()

    def over(j, carry):
        color, trans = carry
        part = parts[j]
        both = jnp.where(upper, pltpu.roll(part, HALF, 0), part)
        return color + trans * part, trans * both

    color, trans = lax.fori_loop(0, nx * groups, over, (zero, one), unroll=nx * groups)
    pieces[x, z] = jnp.where(upper, color, trans)

    def g_copy(j):
        return pltpu.make_async_remote_copy(
            pieces.at[x, z], pieces.at[x, z], g_send.at[j], g_recv.at[z], device_id=at(x, lax.rem(z + j, nz)), device_id_type=MESH
        )

    def f_copy(j, other):
        return pltpu.make_async_remote_copy(
            pieces.at[x, other], pieces.at[x, other], f_send.at[j], f_recv.at[x],
            device_id=at(lax.rem(x + j, nx), z), device_id_type=MESH,
        )

    def arrive(i):
        gap = i // 2 + 1
        return jnp.where(lax.rem(i, 2) == 1, nz - gap, gap)

    def start_g(i, _):
        g_copy(arrive(nz - 2 - i)).start()
        return 0

    lax.fori_loop(0, nz - 1, start_g, 0)
    for j in range(1, nx):
        f_copy(j, z).start()

    def sent(source, done):
        pltpu.make_async_remote_copy(
            source, source, done, done, device_id=(tile, place), device_id_type=MESH
        ).wait_send()

    every = field.at[pl.ds(0, blocks), 0, pl.ds(0, slices)]

    @pl.when(has_above)
    def _():
        sent(every, halo_send.at[0])

    @pl.when(has_below)
    def _():
        sent(every, halo_send.at[1])

    sent(swap_out, s_send)
    sent(parts.at[others], r_send)

    def pass_on(i, _):
        other = lax.rem(z + arrive(i), nz)
        pltpu.make_async_remote_copy(
            pieces.at[x, other], pieces.at[x, other], g_send.at[other], g_recv.at[other],
            device_id=at(x, other), device_id_type=MESH,
        ).wait_recv()
        for j in range(1, nx):
            f_copy(j, other).start()
        return 0

    lax.fori_loop(0, nz - 1, pass_on, 0)

    def whole(j):
        other = lax.rem(x + j, nx)
        return pltpu.make_async_remote_copy(
            pieces.at[other], pieces.at[other], f_send.at[j], f_recv.at[other],
            device_id=at(other, z), device_id_type=MESH,
        )

    for j in range(1, nx):
        whole(j).wait_recv()

    for b in range(blocks):
        for h in range(bricks):
            first, second = pieces[2 * h, b], pieces[2 * h + 1, b]
            color = jnp.where(upper, first, pltpu.roll(second, HALF, 0))
            trans = jnp.where(upper, pltpu.roll(first, HALF, 0), second)
            spot = (pl.ds(BR * h, BR), pl.ds(BW * b, BW))
            for c in range(3):
                image[(c,) + spot] = emission[c] * color
            image[(3,) + spot] = 1.0 - trans

    def end_g(j, _):
        g_copy(j).wait_send()
        return 0

    lax.fori_loop(1, nz, end_g, 0)
    for j in range(1, nx):
        whole(j).wait_send()


def shards(nt, nx, nz, density, slab_start, slab_count, emission, extinction, edge_gain):
    rows, slices, width = density.shape
    blocks = width // BW
    hbm = pl.BlockSpec(memory_space=pltpu.HBM)
    dma, plain = pltpu.SemaphoreType.DMA, pltpu.SemaphoreType.REGULAR
    return pl.pallas_call(
        functools.partial(render, nt, nx, nz),
        out_shape=pltpu.VMEM((4, rows, width), jnp.float32),
        in_specs=[hbm] * 6,
        out_specs=pl.BlockSpec(memory_space=pltpu.VMEM),
        scratch_shapes=[
            pltpu.SMEM(slab_start.shape, jnp.int32),
            pltpu.SMEM(slab_count.shape, jnp.int32),
            pltpu.SMEM(emission.shape, jnp.float32),
            pltpu.SMEM(extinction.shape, jnp.float32),
            pltpu.SMEM(edge_gain.shape, jnp.float32),
            pltpu.VMEM((blocks + 2, rows + 2, slices + PAD, BW), jnp.float32),
            pltpu.VMEM((nz // 2, 2 * rows // BR, BR, BW), jnp.float32),
            pltpu.VMEM((nz // 2, 2 * rows // BR, BR, BW), jnp.float32),
            pltpu.VMEM((nz // 2, nx, BR, BW), jnp.float32),
            pltpu.VMEM((nx * nz // 2, BR, BW), jnp.float32),
            pltpu.VMEM((nx, nz, BR, BW), jnp.float32),
            dma((5,)),
            dma((blocks,)),
            dma((2,)),
            dma((2, blocks)),
            plain(((nz // 2 // REACH).bit_length() - 1,)),
            dma,
            dma((nz // 2,)),
            dma,
            dma,
            dma((nz,)),
            dma((nz,)),
            dma((nx,)),
            dma((nx,)),
            dma,
        ],
        compiler_params=pltpu.CompilerParams(
            collective_id=0, has_side_effects=True, vmem_limit_bytes=56 * 1024 * 1024
        ),
        name="render",
    )(density, slab_start, slab_count, emission, extinction, edge_gain)


def solution(mesh):
    placed = (
        P("tile", "depth", None),
        P("tile", "depth", None),
        P("tile", "depth", None),
        P(),
        P(),
        P(),
    )
    nt, nd = mesh.shape["tile"], mesh.shape["depth"]
    nz = 16
    return jax.shard_map(
        functools.partial(shards, nt, nd // nz, nz),
        mesh=mesh,
        in_specs=placed,
        out_specs=P(None, "tile", None),
        check_vma=False,
    )
```

```python
import functools
import math

import jax
import jax.numpy as jnp
from jax import lax
from jax.experimental import pallas as pl
from jax.experimental.pallas import tpu as pltpu
from jax.sharding import PartitionSpec as P

MESH = pl.DeviceIdType.MESH
BR, BW = 8, 128
HALF = BR // 2
PAD = 8
REACH = 2

AHEAD = 2

def render(
    nt, nx, nz, density, start_in, count_in, emission_in, extinction_in, edge_gain_in, image,
    start, count, emission, extinction, edge_gain, field, swap_out, swap_in, states, parts, pieces,
    small_sem, load_sem, halo_send, halo_recv, heard, s_send, s_recv, r_send, r_recv, g_send, g_recv, f_send, f_recv, o_sem,
):
    rows, slices, width = density.shape
    blocks = width // BW
    bricks = rows // BR
    tile = lax.axis_index("tile")
    place = lax.axis_index("depth")
    x, z = place // nz, lax.rem(place, nz)
    groups = nz // 2
    group, member = z // 2, lax.rem(z, 2)
    partner = z + 1 - 2 * member
    has_above, has_below = tile > 0, tile < nt - 1
    above, below = jnp.where(has_above, tile - 1, tile + 1), jnp.where(has_below, tile + 1, tile - 1)

    def at(px, pz):
        return (tile, px * nz + pz)

    def along(dz):
        return lax.rem(z + dz + nz, nz)

    barrier = pltpu.get_barrier_semaphore()

    @pl.when(has_above)
    def _():
        pl.semaphore_signal(barrier, inc=1, device_id=(above, place), device_id_type=MESH)

    @pl.when(has_below)
    def _():
        pl.semaphore_signal(barrier, inc=1, device_id=(below, place), device_id_type=MESH)

    for dz in range(-REACH, REACH + 1):
        for dx in range(nx):
            if dx or dz:
                pl.semaphore_signal(
                    barrier, inc=1, device_id=at(lax.rem(x + dx, nx), along(dz)), device_id_type=MESH
                )

    small = [
        pltpu.make_async_copy(source, target, small_sem.at[i])
        for i, (source, target) in enumerate((
            (start_in, start), (count_in, count), (emission_in, emission),
            (extinction_in, extinction), (edge_gain_in, edge_gain),
        ))
    ]
    for copy in small:
        copy.start()

    def load(b):
        return pltpu.make_async_copy(
            density.at[:, :, pl.ds(pl.multiple_of(b * BW, BW), BW)],
            field.at[b + 1, pl.ds(1, rows), pl.ds(0, slices)],
            load_sem.at[b],
        )

    def start_load(b, _):
        load(b).start()
        return 0

    lax.fori_loop(0, blocks, start_load, 0)
    zeros = jnp.zeros((rows + 2, slices + PAD, BW), jnp.float32)
    field[0] = zeros
    field[blocks + 1] = zeros
    edge = jnp.zeros((blocks, slices, BW), jnp.float32)

    @pl.when(jnp.logical_not(has_above))
    def _():
        field[pl.ds(1, blocks), 0, pl.ds(0, slices)] = edge

    @pl.when(jnp.logical_not(has_below))
    def _():
        field[pl.ds(1, blocks), rows + 1, pl.ds(0, slices)] = edge


    def turn(i):
        gap = groups // 2 - (i + 1) // 2
        return lax.rem(group + jnp.where(lax.rem(i, 2) == 1, gap, groups - gap), groups)

    def block(i):
        return 2 * turn(lax.rem(i, groups)) + jnp.where(i < groups, 1 - member, member)

    def halo_up(b):
        return pltpu.make_async_remote_copy(
            density.at[0, :, pl.ds(pl.multiple_of(b * BW, BW), BW)],
            field.at[b + 1, rows + 1, pl.ds(0, slices)],
            halo_send.at[0],
            halo_recv.at[0, b],
            device_id=(above, place),
            device_id_type=MESH,
        )

    def halo_down(b):
        return pltpu.make_async_remote_copy(
            density.at[rows - 1, :, pl.ds(pl.multiple_of(b * BW, BW), BW)],
            field.at[b + 1, 0, pl.ds(0, slices)],
            halo_send.at[1],
            halo_recv.at[1, b],
            device_id=(below, place),
            device_id_type=MESH,
        )

    def start_halo(i, _):
        b = block(i)

        @pl.when(has_above)
        def _():
            halo_up(b).start()

        @pl.when(has_below)
        def _():
            halo_down(b).start()

        return 0

    pl.semaphore_wait(barrier, nx * (2 * REACH + 1) + jnp.where(jnp.logical_and(has_above, has_below), 1, 0))
    lax.fori_loop(0, blocks, start_halo, 0)
    rounds = [REACH * 2**i for i in range((nz // 2 // REACH).bit_length() - 1)]
    for i, far in enumerate(rounds):
        if i:
            pl.semaphore_wait(heard.at[i - 1], 2)
        for dz in (-far, far):
            pl.semaphore_signal(heard.at[i], inc=1, device_id=at(x, along(dz)), device_id_type=MESH)

    def end_load(b, _):
        load(b).wait()
        return 0

    lax.fori_loop(0, blocks, end_load, 0)
    for copy in small:
        copy.wait()

    lane = lax.broadcasted_iota(jnp.int32, (BR, BW), 1)
    first_lane, last_lane = lane == 0, lane == BW - 1
    sub = lax.broadcasted_iota(jnp.int32, (BR, BW), 0)
    upper = sub < HALF
    rate = extinction[0] * (-math.log2(math.e) / (slices * nx * nz))
    gain = edge_gain[0] * 0.25
    zero, one = jnp.zeros((BR, BW), jnp.float32), jnp.ones((BR, BW), jnp.float32)

    def march(b):
        stride = slices + PAD
        flat = [field.at[b + j].reshape((rows + 2) * stride, BW) for j in range(3)]
        ranges = [(start[h, 0, b], start[h, 0, b] + count[h, 0, b]) for h in range(bricks)]

        def step(k, carry):
            result = []
            for h in range(bricks):
                total, trans, color = carry[h]
                base = (BR * h + 1) * stride + k
                left, mid, right = (f[pl.ds(base, BR, stride=stride)] for f in flat)
                up = flat[1][pl.ds(base - stride, BR, stride=stride)]
                down = flat[1][pl.ds(base + stride, BR, stride=stride)]
                before = pltpu.roll(jnp.where(last_lane, left, mid), 1, 1)
                after = pltpu.roll(jnp.where(first_lane, right, mid), BW - 1, 1)
                grad_y, grad_x = down - up, after - before
                source = mid + gain * (grad_y * grad_y + grad_x * grad_x)
                low, high = ranges[h]
                live = jnp.logical_and(low <= k, k < high)
                total = total + jnp.where(live, rate, 0.0) * mid
                later = jnp.exp2(total)
                result.append((total, later, color + (trans - later) * source))
            return tuple(result)

        done = lax.fori_loop(0, slices, step, ((zero, one, zero),) * bricks, unroll=slices)
        return [(color, trans) for _, trans, color in done]

    def marched(b):
        @pl.when(has_below)
        def _():
            halo_up(b).wait_recv()

        @pl.when(has_above)
        def _():
            halo_down(b).wait_recv()

        return march(b)

    def s_copy(g):
        return pltpu.make_async_remote_copy(
            swap_out.at[g], swap_in.at[g], s_send, s_recv.at[g], device_id=at(x, partner), device_id_type=MESH
        )

    def for_partner(i, _):
        g = turn(i)
        for h, (color, trans) in enumerate(marched(2 * g + 1 - member)):
            swap_out[g, 2 * h] = color
            swap_out[g, 2 * h + 1] = trans
        s_copy(g).start()
        return 0

    def r_copy(q, g):
        return pltpu.make_async_remote_copy(
            states.at[g, q], parts.at[x * groups + group], r_send, r_recv,
            device_id=at(q, 2 * g + member), device_id_type=MESH,
        )

    in_front = member == 0
    order = sorted(range(1, nx), key=lambda j: -min(j, nx - j))

    def prepare(i, _):
        g = turn(i)
        mine = marched(2 * g + member)
        s_copy(g).wait_recv()
        for h, (color, trans) in enumerate(mine):
            its_color, its_trans = swap_in[g, 2 * h], swap_in[g, 2 * h + 1]
            color = jnp.where(in_front, color + trans * its_color, its_color + its_trans * color)
            trans = trans * its_trans
            states[g, 2 * h] = jnp.where(upper, color, pltpu.roll(trans, HALF, 0))
            states[g, 2 * h + 1] = jnp.where(upper, pltpu.roll(color, HALF, 0), trans)
        return 0

    def hand_out(i, _):
        g = turn(i)
        for j in order:
            r_copy(lax.rem(x + j, nx), g).start()

        @pl.when(g != group)
        def _():
            r_copy(x, g).start()

        return 0

    def for_owners(i, _):
        prepare(i, 0)
        return hand_out(i, 0)

    lax.fori_loop(0, groups, for_partner, 0)
    lax.fori_loop(0, AHEAD, prepare, 0)
    pl.semaphore_wait(heard.at[len(rounds) - 1], 2)
    lax.fori_loop(0, AHEAD, hand_out, 0)
    lax.fori_loop(AHEAD, groups, for_owners, 0)
    parts[x * groups + group] = states[group, x]

    others = pl.ds(0, nx * groups - 1)
    pltpu.make_async_remote_copy(
        parts.at[others], parts.at[others], o_sem, r_recv, device_id=at(lax.rem(x + 1, nx), z), device_id_type=MESH
    ).wait_recv()

    def over(j, carry):
        color, trans = carry
        part = parts[j]
        both = jnp.where(upper, pltpu.roll(part, HALF, 0), part)
        return color + trans * part, trans * both

    color, trans = lax.fori_loop(0, nx * groups, over, (zero, one), unroll=nx * groups)
    pieces[x, z] = jnp.where(upper, color, trans)

    def g_copy(j):
        return pltpu.make_async_remote_copy(
            pieces.at[x, z], pieces.at[x, z], g_send, g_recv.at[z], device_id=at(x, lax.rem(z + j, nz)), device_id_type=MESH
        )

    def f_copy(j, other):
        return pltpu.make_async_remote_copy(
            pieces.at[x, other], pieces.at[x, other], f_send.at[j], f_recv.at[x],
            device_id=at(lax.rem(x + j, nx), z), device_id_type=MESH,
        )

    def arrive(i):
        gap = i // 2 + 1
        return jnp.where(lax.rem(i, 2) == 1, nz - gap, gap)

    def start_g(i, _):
        g_copy(arrive(nz - 2 - i)).start()
        return 0

    lax.fori_loop(0, nz - 1, start_g, 0)
    for j in order:
        f_copy(j, z).start()

    def sent(source, done):
        pltpu.make_async_remote_copy(
            source, source, done, done, device_id=(tile, place), device_id_type=MESH
        ).wait_send()

    every = field.at[pl.ds(0, blocks), 0, pl.ds(0, slices)]

    @pl.when(has_above)
    def _():
        sent(every, halo_send.at[0])

    @pl.when(has_below)
    def _():
        sent(every, halo_send.at[1])

    sent(swap_out, s_send)
    sent(parts.at[others], r_send)

    def pass_on(i, _):
        other = lax.rem(z + arrive(i), nz)
        pltpu.make_async_remote_copy(
            pieces.at[x, other], pieces.at[x, other], g_send, g_recv.at[other],
            device_id=at(x, other), device_id_type=MESH,
        ).wait_recv()
        for j in order:
            f_copy(j, other).start()
        return 0

    lax.fori_loop(0, nz - 1, pass_on, 0)
    sent(pieces.at[0, pl.ds(0, nz - 1)], g_send)

    def whole(j):
        other = lax.rem(x + j, nx)
        return pltpu.make_async_remote_copy(
            pieces.at[other], pieces.at[other], f_send.at[j], f_recv.at[other],
            device_id=at(other, z), device_id_type=MESH,
        )

    for j in range(1, nx):
        whole(j).wait_recv()

    for b in range(blocks):
        for h in range(bricks):
            first, second = pieces[2 * h, b], pieces[2 * h + 1, b]
            color = jnp.where(upper, first, pltpu.roll(second, HALF, 0))
            trans = jnp.where(upper, pltpu.roll(first, HALF, 0), second)
            spot = (pl.ds(BR * h, BR), pl.ds(BW * b, BW))
            for c in range(3):
                image[(c,) + spot] = emission[c] * color
            image[(3,) + spot] = 1.0 - trans

    for j in range(1, nx):
        whole(j).wait_send()


def shards(nt, nx, nz, density, slab_start, slab_count, emission, extinction, edge_gain):
    rows, slices, width = density.shape
    blocks = width // BW
    hbm = pl.BlockSpec(memory_space=pltpu.HBM)
    dma, plain = pltpu.SemaphoreType.DMA, pltpu.SemaphoreType.REGULAR
    return pl.pallas_call(
        functools.partial(render, nt, nx, nz),
        out_shape=pltpu.VMEM((4, rows, width), jnp.float32),
        in_specs=[hbm] * 6,
        out_specs=pl.BlockSpec(memory_space=pltpu.VMEM),
        scratch_shapes=[
            pltpu.SMEM(slab_start.shape, jnp.int32),
            pltpu.SMEM(slab_count.shape, jnp.int32),
            pltpu.SMEM(emission.shape, jnp.float32),
            pltpu.SMEM(extinction.shape, jnp.float32),
            pltpu.SMEM(edge_gain.shape, jnp.float32),
            pltpu.VMEM((blocks + 2, rows + 2, slices + PAD, BW), jnp.float32),
            pltpu.VMEM((nz // 2, 2 * rows // BR, BR, BW), jnp.float32),
            pltpu.VMEM((nz // 2, 2 * rows // BR, BR, BW), jnp.float32),
            pltpu.VMEM((nz // 2, nx, BR, BW), jnp.float32),
            pltpu.VMEM((nx * nz // 2, BR, BW), jnp.float32),
            pltpu.VMEM((nx, nz, BR, BW), jnp.float32),
            dma((5,)),
            dma((blocks,)),
            dma((2,)),
            dma((2, blocks)),
            plain(((nz // 2 // REACH).bit_length() - 1,)),
            dma,
            dma((nz // 2,)),
            dma,
            dma,
            dma,
            dma((nz,)),
            dma((nx,)),
            dma((nx,)),
            dma,
        ],
        compiler_params=pltpu.CompilerParams(
            collective_id=0, has_side_effects=True, vmem_limit_bytes=56 * 1024 * 1024
        ),
        name="render",
    )(density, slab_start, slab_count, emission, extinction, edge_gain)


def solution(mesh):
    placed = (
        P("tile", "depth", None),
        P("tile", "depth", None),
        P("tile", "depth", None),
        P(),
        P(),
        P(),
    )
    nt, nd = mesh.shape["tile"], mesh.shape["depth"]
    nz = 16
    return jax.shard_map(
        functools.partial(shards, nt, nd // nz, nz),
        mesh=mesh,
        in_specs=placed,
        out_specs=P(None, "tile", None),
        check_vma=False,
    )
```

```python
import functools
import math

import jax
import jax.numpy as jnp
from jax import lax
from jax.experimental import pallas as pl
from jax.experimental.pallas import tpu as pltpu
from jax.sharding import PartitionSpec as P

MESH = pl.DeviceIdType.MESH
BR, BW = 8, 128
HALF = BR // 2
PAD = 8
REACH = 4

AHEAD = 7

def render(
    nt, nx, nz, density, start_in, count_in, emission_in, extinction_in, edge_gain_in, image,
    start, count, emission, extinction, edge_gain, field, swap_out, swap_in, mine, states, parts, pieces,
    small_sem, load_sem, halo_send, halo_recv, heard, s_send, s_recv, r_send, r_recv, g_send, g_recv, f_send, f_recv, o_sem,
):
    rows, slices, width = density.shape
    blocks = width // BW
    bricks = rows // BR
    tile = lax.axis_index("tile")
    place = lax.axis_index("depth")
    x, z = place // nz, lax.rem(place, nz)
    groups = nz // 2
    group, member = z // 2, lax.rem(z, 2)
    partner = z + 1 - 2 * member
    has_above, has_below = tile > 0, tile < nt - 1
    above, below = jnp.where(has_above, tile - 1, tile + 1), jnp.where(has_below, tile + 1, tile - 1)

    def at(px, pz):
        return (tile, px * nz + pz)

    def along(dz):
        return lax.rem(z + dz + nz, nz)

    barrier = pltpu.get_barrier_semaphore()

    @pl.when(has_above)
    def _():
        pl.semaphore_signal(barrier, inc=1, device_id=(above, place), device_id_type=MESH)

    @pl.when(has_below)
    def _():
        pl.semaphore_signal(barrier, inc=1, device_id=(below, place), device_id_type=MESH)

    near = [(dx, dz) for dx in range(nx) for dz in range(-REACH, REACH + 1) if dx or dz]
    for dx, dz in sorted(near, key=lambda way: -min(way[0], nx - way[0]) - abs(way[1])):
        pl.semaphore_signal(
            barrier, inc=1, device_id=at(lax.rem(x + dx, nx), along(dz)), device_id_type=MESH
        )

    small = [
        pltpu.make_async_copy(source, target, small_sem.at[i])
        for i, (source, target) in enumerate((
            (start_in, start), (count_in, count), (emission_in, emission),
            (extinction_in, extinction), (edge_gain_in, edge_gain),
        ))
    ]
    for copy in small:
        copy.start()

    def load(b):
        return pltpu.make_async_copy(
            density.at[:, :, pl.ds(pl.multiple_of(b * BW, BW), BW)],
            field.at[b + 1, pl.ds(1, rows), pl.ds(0, slices)],
            load_sem.at[b],
        )

    def start_load(b, _):
        load(b).start()
        return 0

    lax.fori_loop(0, blocks, start_load, 0)
    zeros = jnp.zeros((rows + 2, slices + PAD, BW), jnp.float32)
    field[0] = zeros
    field[blocks + 1] = zeros
    edge = jnp.zeros((blocks, slices, BW), jnp.float32)

    @pl.when(jnp.logical_not(has_above))
    def _():
        field[pl.ds(1, blocks), 0, pl.ds(0, slices)] = edge

    @pl.when(jnp.logical_not(has_below))
    def _():
        field[pl.ds(1, blocks), rows + 1, pl.ds(0, slices)] = edge


    def turn(i):
        gap = groups // 2 - (i + 1) // 2
        return lax.rem(group + jnp.where(lax.rem(i, 2) == 1, gap, groups - gap), groups)

    def block(i):
        return 2 * turn(lax.rem(i, groups)) + jnp.where(i < groups, 1 - member, member)

    def halo_up(b):
        return pltpu.make_async_remote_copy(
            density.at[0, :, pl.ds(pl.multiple_of(b * BW, BW), BW)],
            field.at[b + 1, rows + 1, pl.ds(0, slices)],
            halo_send.at[0],
            halo_recv.at[0, b],
            device_id=(above, place),
            device_id_type=MESH,
        )

    def halo_down(b):
        return pltpu.make_async_remote_copy(
            density.at[rows - 1, :, pl.ds(pl.multiple_of(b * BW, BW), BW)],
            field.at[b + 1, 0, pl.ds(0, slices)],
            halo_send.at[1],
            halo_recv.at[1, b],
            device_id=(below, place),
            device_id_type=MESH,
        )

    def start_halo(i, _):
        b = block(i)

        @pl.when(has_above)
        def _():
            halo_up(b).start()

        @pl.when(has_below)
        def _():
            halo_down(b).start()

        return 0

    pl.semaphore_wait(barrier, nx * (2 * REACH + 1) + jnp.where(jnp.logical_and(has_above, has_below), 1, 0))
    lax.fori_loop(0, blocks, start_halo, 0)
    rounds = [REACH * 2**i for i in range((nz // 2 // REACH).bit_length() - 1)]
    for i, far in enumerate(rounds):
        if i:
            pl.semaphore_wait(heard.at[i - 1], 2)
        for dz in (-far, far):
            pl.semaphore_signal(heard.at[i], inc=1, device_id=at(x, along(dz)), device_id_type=MESH)

    def end_load(b, _):
        load(b).wait()
        return 0

    lax.fori_loop(0, blocks, end_load, 0)
    for copy in small:
        copy.wait()

    lane = lax.broadcasted_iota(jnp.int32, (BR, BW), 1)
    first_lane, last_lane = lane == 0, lane == BW - 1
    sub = lax.broadcasted_iota(jnp.int32, (BR, BW), 0)
    upper = sub < HALF
    rate = extinction[0] * (-math.log2(math.e) / (slices * nx * nz))
    gain = edge_gain[0] * 0.25
    zero, one = jnp.zeros((BR, BW), jnp.float32), jnp.ones((BR, BW), jnp.float32)

    def march(b):
        stride = slices + PAD
        flat = [field.at[b + j].reshape((rows + 2) * stride, BW) for j in range(3)]
        ranges = [(start[h, 0, b], start[h, 0, b] + count[h, 0, b]) for h in range(bricks)]

        def step(k, carry):
            result = []
            for h in range(bricks):
                total, trans, color = carry[h]
                base = (BR * h + 1) * stride + k
                left, mid, right = (f[pl.ds(base, BR, stride=stride)] for f in flat)
                up = flat[1][pl.ds(base - stride, BR, stride=stride)]
                down = flat[1][pl.ds(base + stride, BR, stride=stride)]
                before = pltpu.roll(jnp.where(last_lane, left, mid), 1, 1)
                after = pltpu.roll(jnp.where(first_lane, right, mid), BW - 1, 1)
                grad_y, grad_x = down - up, after - before
                source = mid + gain * (grad_y * grad_y + grad_x * grad_x)
                low, high = ranges[h]
                live = jnp.logical_and(low <= k, k < high)
                total = total + jnp.where(live, rate, 0.0) * mid
                later = jnp.exp2(total)
                result.append((total, later, color + (trans - later) * source))
            return tuple(result)

        done = lax.fori_loop(0, slices, step, ((zero, one, zero),) * bricks, unroll=slices)
        return [(color, trans) for _, trans, color in done]

    def marched(b):
        @pl.when(has_below)
        def _():
            halo_up(b).wait_recv()

        @pl.when(has_above)
        def _():
            halo_down(b).wait_recv()

        return march(b)

    def s_copy(g):
        return pltpu.make_async_remote_copy(
            swap_out.at[g], swap_in.at[g], s_send, s_recv.at[g], device_id=at(x, partner), device_id_type=MESH
        )

    def for_partner(i, _):
        g = turn(i)
        for h, (color, trans) in enumerate(marched(2 * g + 1 - member)):
            swap_out[g, 2 * h] = color
            swap_out[g, 2 * h + 1] = trans
        s_copy(g).start()
        return 0

    def r_copy(q, g):
        return pltpu.make_async_remote_copy(
            states.at[g, q], parts.at[x * groups + group], r_send, r_recv,
            device_id=at(q, 2 * g + member), device_id_type=MESH,
        )

    in_front = member == 0
    order = sorted(range(1, nx), key=lambda j: -min(j, nx - j))

    def for_self(i, _):
        g = turn(i)
        for h, (color, trans) in enumerate(marched(2 * g + member)):
            mine[g, 2 * h] = color
            mine[g, 2 * h + 1] = trans
        return 0

    def hand_out(i, _):
        g = turn(i)
        s_copy(g).wait_recv()
        for h in range(bricks):
            color, trans = mine[g, 2 * h], mine[g, 2 * h + 1]
            its_color, its_trans = swap_in[g, 2 * h], swap_in[g, 2 * h + 1]
            color = jnp.where(in_front, color + trans * its_color, its_color + its_trans * color)
            trans = trans * its_trans
            states[g, 2 * h] = jnp.where(upper, color, pltpu.roll(trans, HALF, 0))
            states[g, 2 * h + 1] = jnp.where(upper, pltpu.roll(color, HALF, 0), trans)
        for j in order:
            r_copy(lax.rem(x + j, nx), g).start()

        @pl.when(g != group)
        def _():
            r_copy(x, g).start()

        return 0

    def for_owners(i, _):
        for_self(i, 0)
        return hand_out(i, 0)

    lax.fori_loop(0, groups, for_partner, 0)
    lax.fori_loop(0, AHEAD, for_self, 0)
    pl.semaphore_wait(heard.at[len(rounds) - 1], 2)
    lax.fori_loop(0, AHEAD, hand_out, 0)
    lax.fori_loop(AHEAD, groups, for_owners, 0)
    parts[x * groups + group] = states[group, x]

    others = pl.ds(0, nx * groups - 1)
    pltpu.make_async_remote_copy(
        parts.at[others], parts.at[others], o_sem, r_recv, device_id=at(lax.rem(x + 1, nx), z), device_id_type=MESH
    ).wait_recv()

    def over(j, carry):
        color, trans = carry
        part = parts[j]
        both = jnp.where(upper, pltpu.roll(part, HALF, 0), part)
        return color + trans * part, trans * both

    color, trans = lax.fori_loop(0, nx * groups, over, (zero, one), unroll=nx * groups)
    pieces[x, z] = jnp.where(upper, color, trans)

    def g_copy(j):
        return pltpu.make_async_remote_copy(
            pieces.at[x, z], pieces.at[x, z], g_send, g_recv.at[z], device_id=at(x, lax.rem(z + j, nz)), device_id_type=MESH
        )

    def f_copy(j, other):
        return pltpu.make_async_remote_copy(
            pieces.at[x, other], pieces.at[x, other], f_send.at[j], f_recv.at[x],
            device_id=at(lax.rem(x + j, nx), z), device_id_type=MESH,
        )

    def arrive(i):
        gap = i // 2 + 1
        return jnp.where(lax.rem(i, 2) == 1, nz - gap, gap)

    def start_g(i, _):
        g_copy(arrive(nz - 2 - i)).start()
        return 0

    lax.fori_loop(0, nz - 1, start_g, 0)
    for j in order:
        f_copy(j, z).start()

    def sent(source, done):
        pltpu.make_async_remote_copy(
            source, source, done, done, device_id=(tile, place), device_id_type=MESH
        ).wait_send()

    every = field.at[pl.ds(0, blocks), 0, pl.ds(0, slices)]

    @pl.when(has_above)
    def _():
        sent(every, halo_send.at[0])

    @pl.when(has_below)
    def _():
        sent(every, halo_send.at[1])

    sent(swap_out, s_send)
    sent(parts.at[others], r_send)

    def pass_on(i, _):
        other = lax.rem(z + arrive(i), nz)
        pltpu.make_async_remote_copy(
            pieces.at[x, other], pieces.at[x, other], g_send, g_recv.at[other],
            device_id=at(x, other), device_id_type=MESH,
        ).wait_recv()
        for j in order:
            f_copy(j, other).start()
        return 0

    lax.fori_loop(0, nz - 1, pass_on, 0)
    sent(pieces.at[0, pl.ds(0, nz - 1)], g_send)

    def whole(j):
        other = lax.rem(x + j, nx)
        return pltpu.make_async_remote_copy(
            pieces.at[other], pieces.at[other], f_send.at[j], f_recv.at[other],
            device_id=at(other, z), device_id_type=MESH,
        )

    for j in range(1, nx):
        whole(j).wait_recv()

    for b in range(blocks):
        for h in range(bricks):
            first, second = pieces[2 * h, b], pieces[2 * h + 1, b]
            color = jnp.where(upper, first, pltpu.roll(second, HALF, 0))
            trans = jnp.where(upper, pltpu.roll(first, HALF, 0), second)
            spot = (pl.ds(BR * h, BR), pl.ds(BW * b, BW))
            for c in range(3):
                image[(c,) + spot] = emission[c] * color
            image[(3,) + spot] = 1.0 - trans

    for j in range(1, nx):
        whole(j).wait_send()


def shards(nt, nx, nz, density, slab_start, slab_count, emission, extinction, edge_gain):
    rows, slices, width = density.shape
    blocks = width // BW
    hbm = pl.BlockSpec(memory_space=pltpu.HBM)
    dma, plain = pltpu.SemaphoreType.DMA, pltpu.SemaphoreType.REGULAR
    return pl.pallas_call(
        functools.partial(render, nt, nx, nz),
        out_shape=pltpu.VMEM((4, rows, width), jnp.float32),
        in_specs=[hbm] * 6,
        out_specs=pl.BlockSpec(memory_space=pltpu.VMEM),
        scratch_shapes=[
            pltpu.SMEM(slab_start.shape, jnp.int32),
            pltpu.SMEM(slab_count.shape, jnp.int32),
            pltpu.SMEM(emission.shape, jnp.float32),
            pltpu.SMEM(extinction.shape, jnp.float32),
            pltpu.SMEM(edge_gain.shape, jnp.float32),
            pltpu.VMEM((blocks + 2, rows + 2, slices + PAD, BW), jnp.float32),
            pltpu.VMEM((nz // 2, 2 * rows // BR, BR, BW), jnp.float32),
            pltpu.VMEM((nz // 2, 2 * rows // BR, BR, BW), jnp.float32),
            pltpu.VMEM((nz // 2, 2 * rows // BR, BR, BW), jnp.float32),
            pltpu.VMEM((nz // 2, nx, BR, BW), jnp.float32),
            pltpu.VMEM((nx * nz // 2, BR, BW), jnp.float32),
            pltpu.VMEM((nx, nz, BR, BW), jnp.float32),
            dma((5,)),
            dma((blocks,)),
            dma((2,)),
            dma((2, blocks)),
            plain(((nz // 2 // REACH).bit_length() - 1,)),
            dma,
            dma((nz // 2,)),
            dma,
            dma,
            dma,
            dma((nz,)),
            dma((nx,)),
            dma((nx,)),
            dma,
        ],
        compiler_params=pltpu.CompilerParams(
            collective_id=0, has_side_effects=True, vmem_limit_bytes=56 * 1024 * 1024
        ),
        name="render",
    )(density, slab_start, slab_count, emission, extinction, edge_gain)


def solution(mesh):
    placed = (
        P("tile", "depth", None),
        P("tile", "depth", None),
        P("tile", "depth", None),
        P(),
        P(),
        P(),
    )
    nt, nd = mesh.shape["tile"], mesh.shape["depth"]
    nz = 16
    return jax.shard_map(
        functools.partial(shards, nt, nd // nz, nz),
        mesh=mesh,
        in_specs=placed,
        out_specs=P(None, "tile", None),
        check_vma=False,
    )
```

```python
import functools
import math

import jax
import jax.numpy as jnp
from jax import lax
from jax.experimental import pallas as pl
from jax.experimental.pallas import tpu as pltpu
from jax.sharding import PartitionSpec as P

MESH = pl.DeviceIdType.MESH
BR, BW = 8, 128
HALF = BR // 2
PAD = 8
REACH = 4

AHEAD = 7

def render(
    nt, nx, nz, density, start_in, count_in, emission_in, extinction_in, edge_gain_in, image,
    start, count, emission, extinction, edge_gain, field, swap_out, swap_in, mine, states, parts, pieces,
    small_sem, load_sem, halo_send, halo_recv, heard, s_send, s_recv, r_send, r_recv, g_send, g_recv, f_send, f_recv, o_sem,
):
    rows, slices, width = density.shape
    blocks = width // BW
    bricks = rows // BR
    tile = lax.axis_index("tile")
    place = lax.axis_index("depth")
    x, z = place // nz, lax.rem(place, nz)
    groups = nz // 2
    group, member = z // 2, lax.rem(z, 2)
    partner = z + 1 - 2 * member
    has_above, has_below = tile > 0, tile < nt - 1
    above, below = jnp.where(has_above, tile - 1, tile + 1), jnp.where(has_below, tile + 1, tile - 1)

    def at(px, pz):
        return (tile, px * nz + pz)

    def along(dz):
        return lax.rem(z + dz + nz, nz)

    barrier = pltpu.get_barrier_semaphore()

    @pl.when(has_above)
    def _():
        pl.semaphore_signal(barrier, inc=1, device_id=(above, place), device_id_type=MESH)

    @pl.when(has_below)
    def _():
        pl.semaphore_signal(barrier, inc=1, device_id=(below, place), device_id_type=MESH)

    near = [(dx, dz) for dx in range(nx) for dz in range(-REACH, REACH + 1) if dx or dz]
    for dx, dz in sorted(near, key=lambda way: -min(way[0], nx - way[0]) - abs(way[1])):
        pl.semaphore_signal(
            barrier, inc=1, device_id=at(lax.rem(x + dx, nx), along(dz)), device_id_type=MESH
        )

    small = [
        pltpu.make_async_copy(source, target, small_sem.at[i])
        for i, (source, target) in enumerate((
            (start_in, start), (count_in, count), (emission_in, emission),
            (extinction_in, extinction), (edge_gain_in, edge_gain),
        ))
    ]
    for copy in small:
        copy.start()

    def load(b):
        return pltpu.make_async_copy(
            density.at[:, :, pl.ds(pl.multiple_of(b * BW, BW), BW)],
            field.at[b + 1, pl.ds(1, rows), pl.ds(0, slices)],
            load_sem.at[b],
        )

    def start_load(b, _):
        load(b).start()
        return 0

    lax.fori_loop(0, blocks, start_load, 0)
    zeros = jnp.zeros((rows + 2, slices + PAD, BW), jnp.float32)
    field[0] = zeros
    field[blocks + 1] = zeros
    edge = jnp.zeros((blocks, slices, BW), jnp.float32)

    @pl.when(jnp.logical_not(has_above))
    def _():
        field[pl.ds(1, blocks), 0, pl.ds(0, slices)] = edge

    @pl.when(jnp.logical_not(has_below))
    def _():
        field[pl.ds(1, blocks), rows + 1, pl.ds(0, slices)] = edge


    def turn(i):
        gap = groups // 2 - (i + 1) // 2
        return lax.rem(group + jnp.where(lax.rem(i, 2) == 1, gap, groups - gap), groups)

    def block(i):
        return 2 * turn(lax.rem(i, groups)) + jnp.where(i < groups, 1 - member, member)

    def halo_up(b):
        return pltpu.make_async_remote_copy(
            density.at[0, :, pl.ds(pl.multiple_of(b * BW, BW), BW)],
            field.at[b + 1, rows + 1, pl.ds(0, slices)],
            halo_send.at[0],
            halo_recv.at[0, b],
            device_id=(above, place),
            device_id_type=MESH,
        )

    def halo_down(b):
        return pltpu.make_async_remote_copy(
            density.at[rows - 1, :, pl.ds(pl.multiple_of(b * BW, BW), BW)],
            field.at[b + 1, 0, pl.ds(0, slices)],
            halo_send.at[1],
            halo_recv.at[1, b],
            device_id=(below, place),
            device_id_type=MESH,
        )

    def start_halo(i, _):
        b = block(i)

        @pl.when(has_above)
        def _():
            halo_up(b).start()

        @pl.when(has_below)
        def _():
            halo_down(b).start()

        return 0

    pl.semaphore_wait(barrier, nx * (2 * REACH + 1) + jnp.where(jnp.logical_and(has_above, has_below), 1, 0))
    rounds = [REACH * 2**i for i in range((nz // 2 // REACH).bit_length() - 1)]
    for i, far in enumerate(rounds):
        if i:
            pl.semaphore_wait(heard.at[i - 1], 2)
        for dz in (-far, far):
            pl.semaphore_signal(heard.at[i], inc=1, device_id=at(x, along(dz)), device_id_type=MESH)
        if i == 0:
            lax.fori_loop(0, blocks, start_halo, 0)

    def end_load(b, _):
        load(b).wait()
        return 0

    lax.fori_loop(0, blocks, end_load, 0)
    for copy in small:
        copy.wait()

    lane = lax.broadcasted_iota(jnp.int32, (BR, BW), 1)
    first_lane, last_lane = lane == 0, lane == BW - 1
    sub = lax.broadcasted_iota(jnp.int32, (BR, BW), 0)
    upper = sub < HALF
    rate = extinction[0] * (-math.log2(math.e) / (slices * nx * nz))
    gain = edge_gain[0] * 0.25
    zero, one = jnp.zeros((BR, BW), jnp.float32), jnp.ones((BR, BW), jnp.float32)

    def march(b):
        stride = slices + PAD
        flat = [field.at[b + j].reshape((rows + 2) * stride, BW) for j in range(3)]
        ranges = [(start[h, 0, b], start[h, 0, b] + count[h, 0, b]) for h in range(bricks)]

        def step(k, carry):
            result = []
            for h in range(bricks):
                total, trans, color = carry[h]
                base = (BR * h + 1) * stride + k
                left, mid, right = (f[pl.ds(base, BR, stride=stride)] for f in flat)
                up = flat[1][pl.ds(base - stride, BR, stride=stride)]
                down = flat[1][pl.ds(base + stride, BR, stride=stride)]
                before = pltpu.roll(jnp.where(last_lane, left, mid), 1, 1)
                after = pltpu.roll(jnp.where(first_lane, right, mid), BW - 1, 1)
                grad_y, grad_x = down - up, after - before
                source = mid + gain * (grad_y * grad_y + grad_x * grad_x)
                low, high = ranges[h]
                live = jnp.logical_and(low <= k, k < high)
                total = total + jnp.where(live, rate, 0.0) * mid
                later = jnp.exp2(total)
                result.append((total, later, color + (trans - later) * source))
            return tuple(result)

        done = lax.fori_loop(0, slices, step, ((zero, one, zero),) * bricks, unroll=slices)
        return [(color, trans) for _, trans, color in done]

    def marched(b):
        @pl.when(has_below)
        def _():
            halo_up(b).wait_recv()

        @pl.when(has_above)
        def _():
            halo_down(b).wait_recv()

        return march(b)

    def s_copy(g):
        return pltpu.make_async_remote_copy(
            swap_out.at[g], swap_in.at[g], s_send, s_recv.at[g], device_id=at(x, partner), device_id_type=MESH
        )

    def for_partner(i, _):
        g = turn(i)
        for h, (color, trans) in enumerate(marched(2 * g + 1 - member)):
            swap_out[g, 2 * h] = color
            swap_out[g, 2 * h + 1] = trans
        s_copy(g).start()
        return 0

    def r_copy(q, g):
        return pltpu.make_async_remote_copy(
            states.at[g, q], parts.at[x * groups + group], r_send, r_recv,
            device_id=at(q, 2 * g + member), device_id_type=MESH,
        )

    in_front = member == 0
    order = sorted(range(1, nx), key=lambda j: -min(j, nx - j))

    def for_self(i, _):
        g = turn(i)
        for h, (color, trans) in enumerate(marched(2 * g + member)):
            mine[g, 2 * h] = color
            mine[g, 2 * h + 1] = trans
        return 0

    def hand_out(i, _):
        g = turn(i)
        s_copy(g).wait_recv()
        for h in range(bricks):
            color, trans = mine[g, 2 * h], mine[g, 2 * h + 1]
            its_color, its_trans = swap_in[g, 2 * h], swap_in[g, 2 * h + 1]
            color = jnp.where(in_front, color + trans * its_color, its_color + its_trans * color)
            trans = trans * its_trans
            states[g, 2 * h] = jnp.where(upper, color, pltpu.roll(trans, HALF, 0))
            states[g, 2 * h + 1] = jnp.where(upper, pltpu.roll(color, HALF, 0), trans)
        for j in order:
            r_copy(lax.rem(x + j, nx), g).start()

        @pl.when(g != group)
        def _():
            r_copy(x, g).start()

        return 0

    def for_owners(i, _):
        for_self(i, 0)
        return hand_out(i, 0)

    lax.fori_loop(0, groups, for_partner, 0)
    lax.fori_loop(0, AHEAD, for_self, 0)
    pl.semaphore_wait(heard.at[len(rounds) - 1], 2)
    lax.fori_loop(0, AHEAD, hand_out, 0)
    lax.fori_loop(AHEAD, groups, for_owners, 0)
    parts[x * groups + group] = states[group, x]

    others = pl.ds(0, nx * groups - 1)
    pltpu.make_async_remote_copy(
        parts.at[others], parts.at[others], o_sem, r_recv, device_id=at(lax.rem(x + 1, nx), z), device_id_type=MESH
    ).wait_recv()

    def over(j, carry):
        color, trans = carry
        part = parts[j]
        both = jnp.where(upper, pltpu.roll(part, HALF, 0), part)
        return color + trans * part, trans * both

    color, trans = lax.fori_loop(0, nx * groups, over, (zero, one), unroll=nx * groups)
    pieces[x, z] = jnp.where(upper, color, trans)

    def g_copy(j):
        return pltpu.make_async_remote_copy(
            pieces.at[x, z], pieces.at[x, z], g_send, g_recv.at[z], device_id=at(x, lax.rem(z + j, nz)), device_id_type=MESH
        )

    def f_copy(j, other):
        return pltpu.make_async_remote_copy(
            pieces.at[x, other], pieces.at[x, other], f_send.at[j], f_recv.at[x],
            device_id=at(lax.rem(x + j, nx), z), device_id_type=MESH,
        )

    def arrive(i):
        gap = i // 2 + 1
        return jnp.where(lax.rem(i, 2) == 1, nz - gap, gap)

    def start_g(i, _):
        g_copy(arrive(nz - 2 - i)).start()
        return 0

    lax.fori_loop(0, nz - 1, start_g, 0)
    for j in order:
        f_copy(j, z).start()

    def sent(source, done):
        pltpu.make_async_remote_copy(
            source, source, done, done, device_id=(tile, place), device_id_type=MESH
        ).wait_send()

    every = field.at[pl.ds(0, blocks), 0, pl.ds(0, slices)]

    @pl.when(has_above)
    def _():
        sent(every, halo_send.at[0])

    @pl.when(has_below)
    def _():
        sent(every, halo_send.at[1])

    sent(swap_out, s_send)
    sent(parts.at[others], r_send)

    def pass_on(i, _):
        other = lax.rem(z + arrive(i), nz)
        pltpu.make_async_remote_copy(
            pieces.at[x, other], pieces.at[x, other], g_send, g_recv.at[other],
            device_id=at(x, other), device_id_type=MESH,
        ).wait_recv()
        for j in order:
            f_copy(j, other).start()
        return 0

    lax.fori_loop(0, nz - 1, pass_on, 0)
    sent(pieces.at[0, pl.ds(0, nz - 1)], g_send)

    def whole(j):
        other = lax.rem(x + j, nx)
        return pltpu.make_async_remote_copy(
            pieces.at[other], pieces.at[other], f_send.at[j], f_recv.at[other],
            device_id=at(other, z), device_id_type=MESH,
        )

    for j in range(1, nx):
        whole(j).wait_recv()

    for b in range(blocks):
        for h in range(bricks):
            first, second = pieces[2 * h, b], pieces[2 * h + 1, b]
            color = jnp.where(upper, first, pltpu.roll(second, HALF, 0))
            trans = jnp.where(upper, pltpu.roll(first, HALF, 0), second)
            spot = (pl.ds(BR * h, BR), pl.ds(BW * b, BW))
            for c in range(3):
                image[(c,) + spot] = emission[c] * color
            image[(3,) + spot] = 1.0 - trans

    for j in range(1, nx):
        whole(j).wait_send()


def shards(nt, nx, nz, density, slab_start, slab_count, emission, extinction, edge_gain):
    rows, slices, width = density.shape
    blocks = width // BW
    hbm = pl.BlockSpec(memory_space=pltpu.HBM)
    dma, plain = pltpu.SemaphoreType.DMA, pltpu.SemaphoreType.REGULAR
    return pl.pallas_call(
        functools.partial(render, nt, nx, nz),
        out_shape=pltpu.VMEM((4, rows, width), jnp.float32),
        in_specs=[hbm] * 6,
        out_specs=pl.BlockSpec(memory_space=pltpu.VMEM),
        scratch_shapes=[
            pltpu.SMEM(slab_start.shape, jnp.int32),
            pltpu.SMEM(slab_count.shape, jnp.int32),
            pltpu.SMEM(emission.shape, jnp.float32),
            pltpu.SMEM(extinction.shape, jnp.float32),
            pltpu.SMEM(edge_gain.shape, jnp.float32),
            pltpu.VMEM((blocks + 2, rows + 2, slices + PAD, BW), jnp.float32),
            pltpu.VMEM((nz // 2, 2 * rows // BR, BR, BW), jnp.float32),
            pltpu.VMEM((nz // 2, 2 * rows // BR, BR, BW), jnp.float32),
            pltpu.VMEM((nz // 2, 2 * rows // BR, BR, BW), jnp.float32),
            pltpu.VMEM((nz // 2, nx, BR, BW), jnp.float32),
            pltpu.VMEM((nx * nz // 2, BR, BW), jnp.float32),
            pltpu.VMEM((nx, nz, BR, BW), jnp.float32),
            dma((5,)),
            dma((blocks,)),
            dma((2,)),
            dma((2, blocks)),
            plain(((nz // 2 // REACH).bit_length() - 1,)),
            dma,
            dma((nz // 2,)),
            dma,
            dma,
            dma,
            dma((nz,)),
            dma((nx,)),
            dma((nx,)),
            dma,
        ],
        compiler_params=pltpu.CompilerParams(
            collective_id=0, has_side_effects=True, vmem_limit_bytes=56 * 1024 * 1024
        ),
        name="render",
    )(density, slab_start, slab_count, emission, extinction, edge_gain)


def solution(mesh):
    placed = (
        P("tile", "depth", None),
        P("tile", "depth", None),
        P("tile", "depth", None),
        P(),
        P(),
        P(),
    )
    nt, nd = mesh.shape["tile"], mesh.shape["depth"]
    nz = 16
    return jax.shard_map(
        functools.partial(shards, nt, nd // nz, nz),
        mesh=mesh,
        in_specs=placed,
        out_specs=P(None, "tile", None),
        check_vma=False,
    )
```

```python
import functools
import math

import jax
import jax.numpy as jnp
from jax import lax
from jax.experimental import pallas as pl
from jax.experimental.pallas import tpu as pltpu
from jax.sharding import PartitionSpec as P

MESH = pl.DeviceIdType.MESH
BR, BW = 8, 128
HALF = BR // 2
PAD = 8
REACH = 4

AHEAD = 7
LATE = 4

def render(
    nt, nx, nz, density, start_in, count_in, emission_in, extinction_in, edge_gain_in, image,
    start, count, emission, extinction, edge_gain, field, swap_out, swap_in, mine, states, parts, pieces,
    small_sem, load_sem, halo_send, halo_recv, heard, s_send, s_recv, r_send, r_recv, g_send, g_recv, f_send, f_recv, o_sem,
):
    rows, slices, width = density.shape
    blocks = width // BW
    bricks = rows // BR
    tile = lax.axis_index("tile")
    place = lax.axis_index("depth")
    x, z = place // nz, lax.rem(place, nz)
    groups = nz // 2
    group, member = z // 2, lax.rem(z, 2)
    partner = z + 1 - 2 * member
    has_above, has_below = tile > 0, tile < nt - 1
    above, below = jnp.where(has_above, tile - 1, tile + 1), jnp.where(has_below, tile + 1, tile - 1)

    def at(px, pz):
        return (tile, px * nz + pz)

    def along(dz):
        return lax.rem(z + dz + nz, nz)

    barrier = pltpu.get_barrier_semaphore()

    @pl.when(has_above)
    def _():
        pl.semaphore_signal(barrier, inc=1, device_id=(above, place), device_id_type=MESH)

    @pl.when(has_below)
    def _():
        pl.semaphore_signal(barrier, inc=1, device_id=(below, place), device_id_type=MESH)

    near = [(dx, dz) for dx in range(nx) for dz in range(-REACH, REACH + 1) if dx or dz]
    for dx, dz in sorted(near, key=lambda way: -min(way[0], nx - way[0]) - abs(way[1])):
        pl.semaphore_signal(
            barrier, inc=1, device_id=at(lax.rem(x + dx, nx), along(dz)), device_id_type=MESH
        )

    small = [
        pltpu.make_async_copy(source, target, small_sem.at[i])
        for i, (source, target) in enumerate((
            (start_in, start), (count_in, count), (emission_in, emission),
            (extinction_in, extinction), (edge_gain_in, edge_gain),
        ))
    ]
    for copy in small:
        copy.start()

    def load(b):
        return pltpu.make_async_copy(
            density.at[:, :, pl.ds(pl.multiple_of(b * BW, BW), BW)],
            field.at[b + 1, pl.ds(1, rows), pl.ds(0, slices)],
            load_sem.at[b],
        )

    def start_load(b, _):
        load(b).start()
        return 0

    lax.fori_loop(0, blocks, start_load, 0)
    zeros = jnp.zeros((rows + 2, slices + PAD, BW), jnp.float32)
    field[0] = zeros
    field[blocks + 1] = zeros
    edge = jnp.zeros((blocks, slices, BW), jnp.float32)

    @pl.when(jnp.logical_not(has_above))
    def _():
        field[pl.ds(1, blocks), 0, pl.ds(0, slices)] = edge

    @pl.when(jnp.logical_not(has_below))
    def _():
        field[pl.ds(1, blocks), rows + 1, pl.ds(0, slices)] = edge


    def turn(i):
        gap = groups // 2 - (i + 1) // 2
        return lax.rem(group + jnp.where(lax.rem(i, 2) == 1, gap, groups - gap), groups)

    def block(i):
        return 2 * turn(lax.rem(i, groups)) + jnp.where(i < groups, 1 - member, member)

    def halo_up(b):
        return pltpu.make_async_remote_copy(
            density.at[0, :, pl.ds(pl.multiple_of(b * BW, BW), BW)],
            field.at[b + 1, rows + 1, pl.ds(0, slices)],
            halo_send.at[0],
            halo_recv.at[0, b],
            device_id=(above, place),
            device_id_type=MESH,
        )

    def halo_down(b):
        return pltpu.make_async_remote_copy(
            density.at[rows - 1, :, pl.ds(pl.multiple_of(b * BW, BW), BW)],
            field.at[b + 1, 0, pl.ds(0, slices)],
            halo_send.at[1],
            halo_recv.at[1, b],
            device_id=(below, place),
            device_id_type=MESH,
        )

    def start_halo(i, _):
        b = block(i)

        @pl.when(has_above)
        def _():
            halo_up(b).start()

        @pl.when(has_below)
        def _():
            halo_down(b).start()

        return 0

    pl.semaphore_wait(barrier, nx * (2 * REACH + 1) + jnp.where(jnp.logical_and(has_above, has_below), 1, 0))
    lax.fori_loop(0, blocks, start_halo, 0)
    rounds = [REACH * 2**i for i in range((nz // 2 // REACH).bit_length() - 1)]
    for i, far in enumerate(rounds):
        if i:
            pl.semaphore_wait(heard.at[i - 1], 2)
        for dz in (-far, far):
            pl.semaphore_signal(heard.at[i], inc=1, device_id=at(x, along(dz)), device_id_type=MESH)

    def end_load(b, _):
        load(b).wait()
        return 0

    lax.fori_loop(0, blocks, end_load, 0)
    for copy in small:
        copy.wait()

    lane = lax.broadcasted_iota(jnp.int32, (BR, BW), 1)
    first_lane, last_lane = lane == 0, lane == BW - 1
    sub = lax.broadcasted_iota(jnp.int32, (BR, BW), 0)
    upper = sub < HALF
    rate = extinction[0] * (-math.log2(math.e) / (slices * nx * nz))
    gain = edge_gain[0] * 0.25
    zero, one = jnp.zeros((BR, BW), jnp.float32), jnp.ones((BR, BW), jnp.float32)

    def march(b):
        stride = slices + PAD
        flat = [field.at[b + j].reshape((rows + 2) * stride, BW) for j in range(3)]
        ranges = [(start[h, 0, b], start[h, 0, b] + count[h, 0, b]) for h in range(bricks)]

        def step(k, carry):
            result = []
            for h in range(bricks):
                total, trans, color = carry[h]
                base = (BR * h + 1) * stride + k
                left, mid, right = (f[pl.ds(base, BR, stride=stride)] for f in flat)
                up = flat[1][pl.ds(base - stride, BR, stride=stride)]
                down = flat[1][pl.ds(base + stride, BR, stride=stride)]
                before = pltpu.roll(jnp.where(last_lane, left, mid), 1, 1)
                after = pltpu.roll(jnp.where(first_lane, right, mid), BW - 1, 1)
                grad_y, grad_x = down - up, after - before
                source = mid + gain * (grad_y * grad_y + grad_x * grad_x)
                low, high = ranges[h]
                live = jnp.logical_and(low <= k, k < high)
                total = total + jnp.where(live, rate, 0.0) * mid
                later = jnp.exp2(total)
                result.append((total, later, color + (trans - later) * source))
            return tuple(result)

        done = lax.fori_loop(0, slices, step, ((zero, one, zero),) * bricks, unroll=slices)
        return [(color, trans) for _, trans, color in done]

    def marched(b):
        @pl.when(has_below)
        def _():
            halo_up(b).wait_recv()

        @pl.when(has_above)
        def _():
            halo_down(b).wait_recv()

        return march(b)

    def s_copy(g):
        return pltpu.make_async_remote_copy(
            swap_out.at[g], swap_in.at[g], s_send, s_recv.at[g], device_id=at(x, partner), device_id_type=MESH
        )

    def for_partner(i, _):
        g = turn(i)
        for h, (color, trans) in enumerate(marched(2 * g + 1 - member)):
            swap_out[g, 2 * h] = color
            swap_out[g, 2 * h + 1] = trans
        s_copy(g).start()
        return 0

    def r_copy(q, g):
        return pltpu.make_async_remote_copy(
            states.at[g, q], parts.at[x * groups + group], r_send, r_recv,
            device_id=at(q, 2 * g + member), device_id_type=MESH,
        )

    in_front = member == 0
    order = sorted(range(1, nx), key=lambda j: -min(j, nx - j))

    def for_self(i, _):
        g = turn(i)
        for h, (color, trans) in enumerate(marched(2 * g + member)):
            mine[g, 2 * h] = color
            mine[g, 2 * h + 1] = trans
        return 0

    def hand_out(i, _):
        g = turn(i)
        s_copy(g).wait_recv()
        for h in range(bricks):
            color, trans = mine[g, 2 * h], mine[g, 2 * h + 1]
            its_color, its_trans = swap_in[g, 2 * h], swap_in[g, 2 * h + 1]
            color = jnp.where(in_front, color + trans * its_color, its_color + its_trans * color)
            trans = trans * its_trans
            states[g, 2 * h] = jnp.where(upper, color, pltpu.roll(trans, HALF, 0))
            states[g, 2 * h + 1] = jnp.where(upper, pltpu.roll(color, HALF, 0), trans)
        for j in order:
            r_copy(lax.rem(x + j, nx), g).start()

        @pl.when(g != group)
        def _():
            r_copy(x, g).start()

        return 0

    def for_owners(i, _):
        for_self(i, 0)
        return hand_out(i, 0)

    lax.fori_loop(0, groups, for_partner, 0)
    lax.fori_loop(0, AHEAD, for_self, 0)
    pl.semaphore_wait(heard.at[len(rounds) - 1], 2)
    lax.fori_loop(0, AHEAD, hand_out, 0)
    lax.fori_loop(AHEAD, groups, for_owners, 0)
    parts[x * groups + group] = states[group, x]

    others = pl.ds(0, nx * groups - 1)
    pltpu.make_async_remote_copy(
        parts.at[others], parts.at[others], o_sem, r_recv, device_id=at(lax.rem(x + 1, nx), z), device_id_type=MESH
    ).wait_recv()

    def over(j, carry):
        color, trans = carry
        part = parts[j]
        both = jnp.where(upper, pltpu.roll(part, HALF, 0), part)
        return color + trans * part, trans * both

    color, trans = lax.fori_loop(0, nx * groups, over, (zero, one), unroll=nx * groups)
    pieces[x, z] = jnp.where(upper, color, trans)

    def g_copy(j):
        return pltpu.make_async_remote_copy(
            pieces.at[x, z], pieces.at[x, z], g_send, g_recv.at[z], device_id=at(x, lax.rem(z + j, nz)), device_id_type=MESH
        )

    def f_copy(j, other, wave):
        return pltpu.make_async_remote_copy(
            pieces.at[x, other], pieces.at[x, other], f_send.at[j], f_recv.at[wave, x],
            device_id=at(lax.rem(x + j, nx), z), device_id_type=MESH,
        )

    def arrive(i):
        gap = i // 2 + 1
        return jnp.where(lax.rem(i, 2) == 1, nz - gap, gap)

    def start_g(i, _):
        g_copy(arrive(nz - 2 - i)).start()
        return 0

    lax.fori_loop(0, nz - 1, start_g, 0)
    for j in order:
        f_copy(j, z, 0).start()

    def sent(source, done):
        pltpu.make_async_remote_copy(
            source, source, done, done, device_id=(tile, place), device_id_type=MESH
        ).wait_send()

    every = field.at[pl.ds(0, blocks), 0, pl.ds(0, slices)]

    @pl.when(has_above)
    def _():
        sent(every, halo_send.at[0])

    @pl.when(has_below)
    def _():
        sent(every, halo_send.at[1])

    sent(swap_out, s_send)
    sent(parts.at[others], r_send)

    def pass_on(i, _):
        other = lax.rem(z + arrive(i), nz)
        pltpu.make_async_remote_copy(
            pieces.at[x, other], pieces.at[x, other], g_send, g_recv.at[other],
            device_id=at(x, other), device_id_type=MESH,
        ).wait_recv()
        for j in order:
            f_copy(j, other, jnp.where(i < nz - 1 - LATE, 0, 1)).start()
        return 0

    lax.fori_loop(0, nz - 1, pass_on, 0)
    sent(pieces.at[0, pl.ds(0, nz - 1)], g_send)

    def whole(j):
        other = lax.rem(x + j, nx)
        return pltpu.make_async_remote_copy(
            pieces.at[other], pieces.at[other], f_send.at[j], f_recv.at[0, other],
            device_id=at(other, z), device_id_type=MESH,
        )

    def landed(count, wave):
        for j in range(1, nx):
            some = pieces.at[0, pl.ds(0, count)]
            pltpu.make_async_remote_copy(
                some, some, f_send.at[j], f_recv.at[wave, lax.rem(x + j, nx)],
                device_id=at(lax.rem(x + j, nx), z), device_id_type=MESH,
            ).wait_recv()

    def assemble(b):
        for h in range(bricks):
            first, second = pieces[2 * h, b], pieces[2 * h + 1, b]
            color = jnp.where(upper, first, pltpu.roll(second, HALF, 0))
            trans = jnp.where(upper, pltpu.roll(first, HALF, 0), second)
            spot = (pl.ds(BR * h, BR), pl.ds(pl.multiple_of(BW * b, BW), BW))
            for c in range(3):
                image[(c,) + spot] = emission[c] * color
            image[(3,) + spot] = 1.0 - trans

    def picture(i, _):
        assemble(lax.rem(z + arrive(i), nz))
        return 0

    landed(nz - LATE, 0)
    assemble(z)
    lax.fori_loop(0, nz - 1 - LATE, picture, 0)
    landed(LATE, 1)
    lax.fori_loop(nz - 1 - LATE, nz - 1, picture, 0, unroll=LATE)

    for j in range(1, nx):
        whole(j).wait_send()


def shards(nt, nx, nz, density, slab_start, slab_count, emission, extinction, edge_gain):
    rows, slices, width = density.shape
    blocks = width // BW
    hbm = pl.BlockSpec(memory_space=pltpu.HBM)
    dma, plain = pltpu.SemaphoreType.DMA, pltpu.SemaphoreType.REGULAR
    return pl.pallas_call(
        functools.partial(render, nt, nx, nz),
        out_shape=pltpu.VMEM((4, rows, width), jnp.float32),
        in_specs=[hbm] * 6,
        out_specs=pl.BlockSpec(memory_space=pltpu.VMEM),
        scratch_shapes=[
            pltpu.SMEM(slab_start.shape, jnp.int32),
            pltpu.SMEM(slab_count.shape, jnp.int32),
            pltpu.SMEM(emission.shape, jnp.float32),
            pltpu.SMEM(extinction.shape, jnp.float32),
            pltpu.SMEM(edge_gain.shape, jnp.float32),
            pltpu.VMEM((blocks + 2, rows + 2, slices + PAD, BW), jnp.float32),
            pltpu.VMEM((nz // 2, 2 * rows // BR, BR, BW), jnp.float32),
            pltpu.VMEM((nz // 2, 2 * rows // BR, BR, BW), jnp.float32),
            pltpu.VMEM((nz // 2, 2 * rows // BR, BR, BW), jnp.float32),
            pltpu.VMEM((nz // 2, nx, BR, BW), jnp.float32),
            pltpu.VMEM((nx * nz // 2, BR, BW), jnp.float32),
            pltpu.VMEM((nx, nz, BR, BW), jnp.float32),
            dma((5,)),
            dma((blocks,)),
            dma((2,)),
            dma((2, blocks)),
            plain(((nz // 2 // REACH).bit_length() - 1,)),
            dma,
            dma((nz // 2,)),
            dma,
            dma,
            dma,
            dma((nz,)),
            dma((nx,)),
            dma((2, nx)),
            dma,
        ],
        compiler_params=pltpu.CompilerParams(
            collective_id=0, has_side_effects=True, vmem_limit_bytes=56 * 1024 * 1024
        ),
        name="render",
    )(density, slab_start, slab_count, emission, extinction, edge_gain)


def solution(mesh):
    placed = (
        P("tile", "depth", None),
        P("tile", "depth", None),
        P("tile", "depth", None),
        P(),
        P(),
        P(),
    )
    nt, nd = mesh.shape["tile"], mesh.shape["depth"]
    nz = 16
    return jax.shard_map(
        functools.partial(shards, nt, nd // nz, nz),
        mesh=mesh,
        in_specs=placed,
        out_specs=P(None, "tile", None),
        check_vma=False,
    )
```
